256 devices in a mesh: dp: 4 (over y_hi, core), seq: 32 (over x, z), tensor: 2 (over y_lo).
Axes of the slice: x: 4, y: 4 (y_hi: 2, y_lo: 2; y = y_hi * 2 + y_lo), z: 8, core: 2. Of those that a mesh axis runs over, the one named last changes fastest.
Arguments:
- latents: bfloat16 [4, 32, 128, 1152], P('dp', 'seq'), may hold values from -6 to 6
- modulation: float32 [4, 6, 1152], P('dp'), may hold values from -3 to 3
- cotangent: bfloat16 [4, 32, 128, 1152], P('dp', 'seq'), may hold values from -6 to 6
- proj_spatial: bfloat16 [1152, 3, 1152], P(None, None, 'tensor'), may hold values from -1 to 1
- out_spatial: bfloat16 [1152, 1152], P(None, 'tensor'), may hold values from -0.1875 to 0.1875
- proj_temporal: bfloat16 [1152, 3, 1152], P(None, None, 'tensor'), may hold values from -1 to 1
- out_temporal: bfloat16 [1152, 1152], P(None, 'tensor'), may hold values from -0.1875 to 0.1875
Outputs:
- block_output: bfloat16 [4, 32, 128, 1152], P('dp', 'seq')
- latent_grad: float32 [4, 32, 128, 1152], P('dp', 'seq')
- out_spatial_grad: float32 [1152, 1152], P(('dp', 'seq'), 'tensor')
- out_temporal_grad: float32 [1152, 1152], P(('dp', 'seq'), 'tensor')
The draws below stay inside these ranges and needn't reach their ends.
All inputs are finite; a program needn't handle non-finite values.
Results may differ from the reference program's by a relative error of at most 0.019.
Values may be sent and summed in bfloat16 or wider, within the bound.
No kernel may reach another device: no remote copies, remote signals or barrier semaphores. Data moves between devices by JAX's collectives and lax.ppermute only.
A program may use at most 128 MiB of HBM per device.

```python
import jax
import jax.numpy as jnp
from jax import lax

HEAD_DIM = 72
D = 1152
PATCHES = 128
CLIPS = 4
FRAMES = 32


def draw_proj_spatial(key, part):
    key = jax.random.fold_in(key, 11)
    base_draw = jax.random.normal(jax.random.fold_in(key, 1), (D, 3, D), jnp.float32) * D ** (-0.5)
    return jnp.clip(base_draw, -1.0, 1.0).astype(jnp.bfloat16)


def draw_proj_temporal(key, part):
    key = jax.random.fold_in(key, 23)
    base_draw = jax.random.normal(jax.random.fold_in(key, 1), (D, 3, D), jnp.float32) * D ** (-0.5)
    return jnp.clip(base_draw, -1.0, 1.0).astype(jnp.bfloat16)


def shard_levels(stream_key, extent, shards, low, high):
    def one(axis_at, parts):
        heights = jax.random.uniform(jax.random.fold_in(jax.random.fold_in(stream_key, 6), axis_at), (parts,), jnp.float32, low / len(shards), high / len(shards))
        return jnp.repeat(jnp.exp(heights), extent[axis_at] // parts).reshape((-1,) + (1,) * (len(extent) - axis_at - 1))

    level = one(*shards[0])
    for cut in shards[1:]:
        level = level * one(*cut)
    return level


def noise(key, extent, width, most, cuts=(), dtype=jnp.bfloat16):
    level = shard_levels(key, extent, cuts, -0.22, 0.18) if cuts else 1.0
    entries = jax.random.normal(key, extent, jnp.float32) * width * level
    return jnp.minimum(jnp.maximum(entries, -most), most).astype(dtype)


def setup_inputs(seed: int = 0) -> dict:
    arg_keys = jax.random.split(jax.random.key(seed), 8)
    return {
        "latents": noise(arg_keys[0], (CLIPS, FRAMES, PATCHES, D), 1.0, 6.0, ((0, 4), (1, 32))),
        "modulation": noise(arg_keys[1], (CLIPS, 6, D), 0.5, 3.0, ((0, 4),), jnp.float32),
        "cotangent": noise(arg_keys[2], (CLIPS, FRAMES, PATCHES, D), 1.0, 6.0, ((0, 4), (1, 32))),
        "proj_spatial": draw_proj_spatial(jax.random.fold_in(arg_keys[7], 71), 0),
        "out_spatial": noise(arg_keys[4], (D, D), D ** -0.5, 0.1875, ((1, 2),)),
        "proj_temporal": draw_proj_temporal(jax.random.fold_in(arg_keys[7], 71), 0),
        "out_temporal": noise(arg_keys[6], (D, D), D ** -0.5, 0.1875, ((1, 2),)),
    }


NORM_EPS = 1e-06
SPATIAL_FORMS = ('bfphe,bfqhe->bfhpq', 'bfhpq,bfqhe->bfphe', 'bfhpq,bfphe->bfqhe')
TEMPORAL_FORMS = ('bfphe,bgphe->bphfg', 'bphfg,bgphe->bfphe', 'bphfg,bfphe->bgphe')

def contract(einsum_form, left_side, right_side):
    return jnp.einsum(einsum_form, left_side.astype(jnp.float32), right_side.astype(jnp.float32))

def matmul(left_side, right_side):
    return jnp.dot(left_side, right_side, preferred_element_type=jnp.float32)

def matmul_left_t(left_side, right_side):
    return jnp.dot(left_side.T, right_side, preferred_element_type=jnp.float32)

def matmul_right_t(left_side, right_side):
    return jnp.dot(left_side, right_side.T, preferred_element_type=jnp.float32)

def norm_mod(values, shift_row, scale_row):
    average = lax.optimization_barrier(jnp.mean(values, axis=-1, keepdims=True))
    centred = values - average
    variance = lax.optimization_barrier(jnp.mean(centred * centred, axis=-1, keepdims=True))
    return centred * lax.rsqrt(variance + NORM_EPS) * (1.0 + scale_row) + shift_row

def norm_back(values, shift_row, scale_row, incoming):
    _, pull_back = jax.vjp(lambda inner_values: norm_mod(inner_values, shift_row, scale_row), values)
    return pull_back(incoming)[0]

def probabilities(queries, keys_in, form_set):
    scores = contract(form_set[0], queries, keys_in) * queries.shape[-1] ** (-0.5)
    top_score = lax.optimization_barrier(jnp.max(scores, axis=-1, keepdims=True))
    raised = jnp.exp(scores - top_score)
    return raised / lax.optimization_barrier(jnp.sum(raised, axis=-1, keepdims=True))

def attend(queries, keys_in, values_in, form_set):
    weights = probabilities(queries, keys_in, form_set).astype(jnp.bfloat16)
    return contract(form_set[1], weights, values_in).astype(jnp.bfloat16)

def attend_back(queries, keys_in, values_in, grad_out, form_set):
    weights = probabilities(queries, keys_in, form_set)
    rounded = weights.astype(jnp.bfloat16)
    grad_weights = contract(form_set[0], grad_out, values_in)
    inner_sum = lax.optimization_barrier(jnp.sum(grad_weights * weights, axis=-1, keepdims=True))
    grad_scores = (weights * (grad_weights - inner_sum) * queries.shape[-1] ** (-0.5)).astype(jnp.bfloat16)
    grad_queries = contract(form_set[1], grad_scores, keys_in).astype(jnp.bfloat16)
    grad_keys = contract(form_set[2], grad_scores, queries).astype(jnp.bfloat16)
    grad_values = contract(form_set[2], rounded, grad_out).astype(jnp.bfloat16)
    return jnp.stack((grad_queries, grad_keys, grad_values), axis=3)

def reference(latents, modulation, cotangent, proj_spatial, out_spatial, proj_temporal, out_temporal):
    clip_count, frame_count, patch_count, model_width = latents.shape
    head_count = model_width // HEAD_DIM
    frame_shape = (clip_count, frame_count, patch_count, 3, head_count, HEAD_DIM)
    head_shape = (clip_count, frame_count, patch_count, head_count, HEAD_DIM)
    mod_rows = modulation[:, :, None, None, :]
    proj_flat_s = proj_spatial.reshape(model_width, 3 * model_width)
    proj_flat_t = proj_temporal.reshape(model_width, 3 * model_width)
    inputs = latents.astype(jnp.float32)
    normed_s = norm_mod(inputs, mod_rows[:, 0], mod_rows[:, 1]).astype(jnp.bfloat16)
    flat_s = normed_s.reshape(-1, model_width)
    packed_s = matmul(flat_s, proj_flat_s).astype(jnp.bfloat16).reshape(frame_shape)
    heads_s = attend(packed_s[:, :, :, 0], packed_s[:, :, :, 1], packed_s[:, :, :, 2], SPATIAL_FORMS)
    heads_flat_s = heads_s.reshape(-1, model_width)
    mixed_s = matmul_right_t(heads_flat_s, out_spatial)
    middle = inputs + mod_rows[:, 2] * mixed_s.reshape(inputs.shape)
    normed_t = norm_mod(middle, mod_rows[:, 3], mod_rows[:, 4]).astype(jnp.bfloat16)
    flat_t = normed_t.reshape(-1, model_width)
    packed_t = matmul(flat_t, proj_flat_t).astype(jnp.bfloat16).reshape(frame_shape)
    heads_t = attend(packed_t[:, :, :, 0], packed_t[:, :, :, 1], packed_t[:, :, :, 2], TEMPORAL_FORMS)
    heads_flat_t = heads_t.reshape(-1, model_width)
    mixed_t = matmul_right_t(heads_flat_t, out_temporal)
    block_output = (middle + mod_rows[:, 5] * mixed_t.reshape(inputs.shape)).astype(jnp.bfloat16)
    upstream = cotangent.astype(jnp.float32)
    scaled_t = (mod_rows[:, 5] * upstream).astype(jnp.bfloat16).reshape(-1, model_width)
    out_temporal_grad = matmul_left_t(scaled_t, heads_flat_t)
    grad_heads_t = matmul(scaled_t, out_temporal).astype(jnp.bfloat16).reshape(head_shape)
    grad_packed_t = attend_back(packed_t[:, :, :, 0], packed_t[:, :, :, 1], packed_t[:, :, :, 2], grad_heads_t, TEMPORAL_FORMS)
    grad_packed_t = grad_packed_t.reshape(-1, 3 * model_width)
    grad_normed_t = matmul_right_t(grad_packed_t, proj_flat_t)
    grad_middle = upstream + norm_back(middle, mod_rows[:, 3], mod_rows[:, 4], grad_normed_t.reshape(inputs.shape))
    scaled_s = (mod_rows[:, 2] * grad_middle).astype(jnp.bfloat16).reshape(-1, model_width)
    out_spatial_grad = matmul_left_t(scaled_s, heads_flat_s)
    grad_heads_s = matmul(scaled_s, out_spatial).astype(jnp.bfloat16).reshape(head_shape)
    grad_packed_s = attend_back(packed_s[:, :, :, 0], packed_s[:, :, :, 1], packed_s[:, :, :, 2], grad_heads_s, SPATIAL_FORMS)
    grad_packed_s = grad_packed_s.reshape(-1, 3 * model_width)
    grad_normed_s = matmul_right_t(grad_packed_s, proj_flat_s)
    latent_grad = grad_middle + norm_back(inputs, mod_rows[:, 0], mod_rows[:, 1], grad_normed_s.reshape(inputs.shape))
    return (block_output, latent_grad, out_spatial_grad, out_temporal_grad)
```

```python
import jax
import jax.numpy as jnp
from jax import lax
from jax.sharding import PartitionSpec as P

HEAD_DIM = 72


NORM_EPS = 1e-06
SPATIAL_FORMS = ("bfphe,bfqhe->bfhpq", "bfhpq,bfqhe->bfphe", "bfhpq,bfphe->bfqhe")
TEMPORAL_FORMS = ("bfphe,bgphe->bphfg", "bphfg,bgphe->bfphe", "bphfg,bfphe->bgphe")


def contract(einsum_form, left_side, right_side):
    return jnp.einsum(einsum_form, left_side, right_side, preferred_element_type=jnp.float32)


def matmul(left_side, right_side):
    return jnp.dot(left_side, right_side, preferred_element_type=jnp.float32)


def matmul_left_t(left_side, right_side):
    return lax.dot_general(
        left_side, right_side, (((0,), (0,)), ((), ())), preferred_element_type=jnp.float32
    )


def matmul_right_t(left_side, right_side):
    return lax.dot_general(
        left_side, right_side, (((1,), (1,)), ((), ())), preferred_element_type=jnp.float32
    )


def norm_mod(values, shift_row, scale_row):
    average = jnp.mean(values, axis=-1, keepdims=True)
    centred = values - average
    variance = jnp.mean(centred * centred, axis=-1, keepdims=True)
    return centred * lax.rsqrt(variance + NORM_EPS) * (1.0 + scale_row) + shift_row


def norm_back(values, shift_row, scale_row, incoming):
    _, pull_back = jax.vjp(
        lambda inner_values: norm_mod(inner_values, shift_row, scale_row), values
    )
    return pull_back(incoming)[0]


def probabilities(queries, keys_in, form_set):
    scores = contract(form_set[0], queries, keys_in) * queries.shape[-1] ** (-0.5)
    top_score = jnp.max(scores, axis=-1, keepdims=True)
    raised = jnp.exp(scores - top_score)
    return raised / jnp.sum(raised, axis=-1, keepdims=True)


def attend(queries, keys_in, values_in, form_set):
    weights = probabilities(queries, keys_in, form_set).astype(jnp.bfloat16)
    return contract(form_set[1], weights, values_in).astype(jnp.bfloat16)


def attend_back(queries, keys_in, values_in, grad_out, form_set):
    weights = probabilities(queries, keys_in, form_set)
    rounded = weights.astype(jnp.bfloat16)
    grad_weights = contract(form_set[0], grad_out, values_in)
    inner_sum = jnp.sum(grad_weights * weights, axis=-1, keepdims=True)
    grad_scores = (weights * (grad_weights - inner_sum) * queries.shape[-1] ** (-0.5)).astype(
        jnp.bfloat16
    )
    grad_queries = contract(form_set[1], grad_scores, keys_in).astype(jnp.bfloat16)
    grad_keys = contract(form_set[2], grad_scores, queries).astype(jnp.bfloat16)
    grad_values = contract(form_set[2], rounded, grad_out).astype(jnp.bfloat16)
    return jnp.stack((grad_queries, grad_keys, grad_values), axis=3)

PAIR = ((0, 1), (1, 0))
CORE_SWAP = ((0, 1), (1, 0), (2, 3), (3, 2))
FAR_SWAP = ((0, 2), (2, 0), (1, 3), (3, 1))


def pair_sum(partial):
    mine = partial.astype(jnp.bfloat16)
    other = lax.ppermute(mine, "tensor", PAIR)
    return mine.astype(jnp.float32) + other.astype(jnp.float32)


def pick(array, index):
    return lax.dynamic_index_in_dim(array, index, 0, keepdims=False)


def gather_heads(heads):
    near = jnp.stack((heads, lax.ppermute(heads, "dp", CORE_SWAP)))
    return jnp.stack((near, lax.ppermute(near, "dp", FAR_SWAP)))


def weight_grad(scaled, heads_all):
    place = lax.axis_index("dp")
    core, far = place % 2, place // 2
    tokens, width = scaled.shape
    cut = scaled.reshape(tokens, 2, 2, width // 4).transpose(2, 1, 0, 3)
    near = jnp.stack((pick(cut, core), lax.ppermute(pick(cut, 1 - core), "dp", CORE_SWAP)), axis=1)
    every = jnp.stack((pick(near, far), lax.ppermute(pick(near, 1 - far), "dp", FAR_SWAP)))
    total = lax.dot_general(
        every.reshape(4 * tokens, width // 4),
        heads_all.reshape(4 * tokens, -1),
        (((0,), (0,)), ((), ())),
        preferred_element_type=jnp.float32,
    )
    seq = lax.axis_index("seq")
    columns = total.shape[1]
    total = total.reshape(2, 2, 2, 2, 2, -1, columns)
    total = total.transpose(4, 1, 3, 0, 2, 5, 6)
    for bit in (0, 3, 1, 4, 2):
        mask = 1 << bit
        swap = [(i, i ^ mask) for i in range(32)]
        mine = (seq >> bit) & 1
        total = total.reshape(2, -1, columns)
        sent = pick(total, 1 - mine).astype(jnp.bfloat16)
        total = pick(total, mine) + lax.ppermute(sent, "seq", swap).astype(jnp.float32)
    return total


def per_device(
    latents, modulation, cotangent, proj_spatial, out_spatial, proj_temporal, out_temporal
):
    clip_count, frame_count, patch_count, model_width = latents.shape
    local_width = out_spatial.shape[1]
    head_count = local_width // HEAD_DIM
    frame_shape = (clip_count, frame_count, patch_count, 3, head_count, HEAD_DIM)
    head_shape = (clip_count, frame_count, patch_count, head_count, HEAD_DIM)
    mod_rows = modulation[:, :, None, None, :]
    proj_flat_s = proj_spatial.reshape(model_width, 3 * local_width)
    proj_flat_t = proj_temporal.reshape(model_width, 3 * local_width)
    inputs = latents.astype(jnp.float32)
    normed_s = norm_mod(inputs, mod_rows[:, 0], mod_rows[:, 1]).astype(jnp.bfloat16)
    flat_s = normed_s.reshape(-1, model_width)
    packed_s = matmul(flat_s, proj_flat_s).astype(jnp.bfloat16).reshape(frame_shape)
    heads_s = attend(
        packed_s[:, :, :, 0], packed_s[:, :, :, 1], packed_s[:, :, :, 2], SPATIAL_FORMS
    )
    heads_flat_s = heads_s.reshape(-1, local_width)
    mixed_s = pair_sum(matmul_right_t(heads_flat_s, out_spatial))
    middle = inputs + mod_rows[:, 2] * mixed_s.reshape(inputs.shape)
    normed_t = norm_mod(middle, mod_rows[:, 3], mod_rows[:, 4]).astype(jnp.bfloat16)
    packed_t = matmul(normed_t.reshape(-1, model_width), proj_flat_t).astype(jnp.bfloat16)
    packed_t = packed_t.reshape(clip_count, frame_count, patch_count, 3 * local_width)
    arrived = lax.all_to_all(packed_t, "seq", split_axis=2, concat_axis=1, tiled=True)
    frames_all = arrived.shape[1]
    patches_loc = arrived.shape[2]
    arrived = arrived.reshape(clip_count, frames_all, patches_loc, 3, head_count, HEAD_DIM)
    heads_t = attend(arrived[:, :, :, 0], arrived[:, :, :, 1], arrived[:, :, :, 2], TEMPORAL_FORMS)
    heads_t = heads_t.reshape(clip_count, frames_all, patches_loc, local_width)
    heads_back = lax.all_to_all(heads_t, "seq", split_axis=1, concat_axis=2, tiled=True)
    heads_flat_t = heads_back.reshape(-1, local_width)
    mixed_t = pair_sum(matmul_right_t(heads_flat_t, out_temporal))
    block_output = (middle + mod_rows[:, 5] * mixed_t.reshape(inputs.shape)).astype(jnp.bfloat16)
    upstream = cotangent.astype(jnp.float32)
    scaled_t = (mod_rows[:, 5] * upstream).astype(jnp.bfloat16).reshape(-1, model_width)
    summed_out_t = weight_grad(scaled_t, gather_heads(heads_flat_t))
    grad_heads_t = matmul(scaled_t, out_temporal).astype(jnp.bfloat16)
    grad_heads_t = grad_heads_t.reshape(clip_count, frame_count, patch_count, local_width)
    grad_moved = lax.all_to_all(grad_heads_t, "seq", split_axis=2, concat_axis=1, tiled=True)
    grad_moved = grad_moved.reshape(clip_count, frames_all, patches_loc, head_count, HEAD_DIM)
    grad_packed_t = attend_back(
        arrived[:, :, :, 0], arrived[:, :, :, 1], arrived[:, :, :, 2], grad_moved, TEMPORAL_FORMS
    )
    grad_packed_t = grad_packed_t.reshape(clip_count, frames_all, patches_loc, 3 * local_width)
    grad_packed_back = lax.all_to_all(grad_packed_t, "seq", split_axis=1, concat_axis=2, tiled=True)
    grad_packed_back = grad_packed_back.reshape(-1, 3 * local_width)
    partial_t = matmul_right_t(grad_packed_back, proj_flat_t)
    grad_normed_t = pair_sum(partial_t)
    grad_middle = upstream + norm_back(
        middle, mod_rows[:, 3], mod_rows[:, 4], grad_normed_t.reshape(inputs.shape)
    )
    scaled_s = (mod_rows[:, 2] * grad_middle).astype(jnp.bfloat16).reshape(-1, model_width)
    summed_out_s = weight_grad(scaled_s, gather_heads(heads_flat_s))
    grad_heads_s = matmul(scaled_s, out_spatial).astype(jnp.bfloat16).reshape(head_shape)
    grad_packed_s = attend_back(
        packed_s[:, :, :, 0],
        packed_s[:, :, :, 1],
        packed_s[:, :, :, 2],
        grad_heads_s,
        SPATIAL_FORMS,
    )
    grad_packed_s = grad_packed_s.reshape(-1, 3 * local_width)
    grad_normed_s = pair_sum(matmul_right_t(grad_packed_s, proj_flat_s))
    latent_grad = grad_middle + norm_back(
        inputs, mod_rows[:, 0], mod_rows[:, 1], grad_normed_s.reshape(inputs.shape)
    )
    return (block_output, latent_grad, summed_out_s, summed_out_t)


def solution(mesh):
    placed = (
        P("dp", "seq", None, None),
        P("dp", None, None),
        P("dp", "seq", None, None),
        P(None, None, "tensor"),
        P(None, "tensor"),
        P(None, None, "tensor"),
        P(None, "tensor"),
    )
    return jax.shard_map(
        per_device,
        mesh=mesh,
        in_specs=placed,
        out_specs=(
            P("dp", "seq", None, None),
            P("dp", "seq", None, None),
            P(("dp", "seq"), "tensor"),
            P(("dp", "seq"), "tensor"),
        ),
        check_vma=False,
    )
```

```python
import functools

import jax
import jax.numpy as jnp
from jax import lax
from jax.experimental import pallas as pl
from jax.experimental.pallas import tpu as pltpu
from jax.sharding import PartitionSpec as P

HEAD_DIM = 72
NORM_EPS = 1e-06
PAIR = ((0, 1), (1, 0))
DP = 4
SEQ = 32
BF = jnp.bfloat16
F32 = jnp.float32
ROWS = 24


def mm(left, right):
    return jnp.dot(left, right, preferred_element_type=F32)


def mm_rt(left, right):
    return lax.dot_general(left, right, (((1,), (1,)), ((), ())), preferred_element_type=F32)


def mm_lt(left, right):
    return lax.dot_general(left, right, (((0,), (0,)), ((), ())), preferred_element_type=F32)


def normalise(values):
    average = jnp.mean(values, axis=-1, keepdims=True)
    centred = values - average
    inverse = lax.rsqrt(jnp.mean(centred * centred, axis=-1, keepdims=True) + NORM_EPS)
    return centred * inverse, inverse


def norm_back(values, scale_row, incoming):
    unit, inverse = normalise(values)
    scaled = incoming * (1.0 + scale_row)
    mean_plain = jnp.mean(scaled, axis=-1, keepdims=True)
    mean_unit = jnp.mean(scaled * unit, axis=-1, keepdims=True)
    return inverse * (scaled - mean_plain - unit * mean_unit)


def stack_heads(values):
    width = values.shape[1]
    owner = lax.broadcasted_iota(jnp.int32, (1, width), 1) // HEAD_DIM
    parts = [values * (owner == head).astype(F32).astype(BF) for head in range(width // HEAD_DIM)]
    return jnp.concatenate(parts, axis=0)


def side_by_side(stacked):
    tokens = stacked.shape[1]
    heads = stacked.shape[0] // tokens
    return jnp.concatenate([stacked[h * tokens : (h + 1) * tokens] for h in range(heads)], axis=1)


def softmax_weights(queries, keys_in, same=None):
    scores = mm_rt(stack_heads(queries), keys_in) * HEAD_DIM**-0.5
    if same is not None:
        scores = jnp.where(same, scores, -1e30)
    raised = jnp.exp(scores - jnp.max(scores, axis=-1, keepdims=True))
    return raised / jnp.sum(raised, axis=-1, keepdims=True)


def attend_back(queries, keys_in, values_in, grad_out, weights):
    grad_stacked = stack_heads(grad_out)
    grad_weights = mm_rt(grad_stacked, values_in)
    inner_sum = jnp.sum(grad_weights * weights, axis=-1, keepdims=True)
    grad_scores = (weights * (grad_weights - inner_sum) * HEAD_DIM**-0.5).astype(BF)
    grad_queries = mm(side_by_side(grad_scores), stack_heads(keys_in)).astype(BF)
    grad_keys = mm_lt(grad_scores, stack_heads(queries)).astype(BF)
    grad_values = mm_lt(weights.astype(BF), grad_stacked).astype(BF)
    return grad_queries, grad_keys, grad_values


def wire_row(index, tokens):
    part, token = index // tokens, index % tokens
    return 16 * (token // 4) + 4 * part + token % 4


def to_wire(parts):
    tokens = parts[0].shape[0]
    rows = 4 * tokens
    held = wire_row(lax.broadcasted_iota(jnp.int32, (1, rows), 1), tokens)
    place = lax.broadcasted_iota(jnp.int32, (rows, rows), 0) == held
    return mm(place.astype(F32).astype(BF), jnp.concatenate(parts, axis=0)).astype(BF)


def from_wire(rows_in):
    rows = rows_in.shape[0]
    tokens = rows // 4
    held = wire_row(lax.broadcasted_iota(jnp.int32, (rows, 1), 0), tokens)
    place = lax.broadcasted_iota(jnp.int32, (rows, rows), 1) == held
    full = mm(place.astype(F32).astype(BF), rows_in).astype(BF)
    return [full[i * tokens : (i + 1) * tokens] for i in range(4)]


def spatial_forward(x_ref, mod_ref, proj_ref, out_ref, packed_ref, weights_ref, heads_ref, mixed_ref):
    unit, _ = normalise(x_ref[...].astype(F32))
    normed = (unit * (1.0 + mod_ref[1:2]) + mod_ref[0:1]).astype(BF)
    queries, keys_in, values_in = [mm(normed, proj_ref[i]).astype(BF) for i in range(3)]
    packed_ref[0] = queries
    packed_ref[1] = keys_in
    packed_ref[2] = values_in
    weights = softmax_weights(queries, keys_in)
    weights_ref[...] = weights
    heads = mm(side_by_side(weights.astype(BF)), stack_heads(values_in)).astype(BF)
    heads_ref[...] = heads
    mixed_ref[...] = mm_rt(heads, out_ref[...]).astype(BF)


def split_columns(scaled, place, held_ref, block_refs):
    wide = scaled.shape[1] // DP
    for i in range(DP):
        held_ref[i] = scaled[:, i * wide : (i + 1) * wide]
    for i in range(DP):
        block_refs[i][...] = held_ref[place ^ i]


def upstream_start(place_ref, cot_ref, mod_ref, out_ref, grad_ref, b0, b1, b2, b3, held_ref):
    scaled = (mod_ref[5:6] * cot_ref[...].astype(F32)).astype(BF)
    grad_ref[...] = mm(scaled, out_ref[...]).astype(BF)
    split_columns(scaled, place_ref[0], held_ref, (b0, b1, b2, b3))


def middle_step(x_ref, mod_ref, mine_ref, other_ref, proj_ref, grad_ref, middle_ref, wire_ref):
    mixed = mine_ref[...].astype(F32) + other_ref[...].astype(F32)
    middle = x_ref[...].astype(F32) + mod_ref[2:3] * mixed
    middle_ref[...] = middle
    unit, _ = normalise(middle)
    normed = (unit * (1.0 + mod_ref[4:5]) + mod_ref[3:4]).astype(BF)
    parts = [mm(normed, proj_ref[i]).astype(BF) for i in range(3)]
    wire_ref[...] = to_wire(parts + [grad_ref[...]])


def temporal_step(arrived_ref, wire_ref):
    queries, keys_in, values_in, grad_out = from_wire(arrived_ref[...])
    tokens = queries.shape[0]
    heads = queries.shape[1] // HEAD_DIM
    row = lax.broadcasted_iota(jnp.int32, (heads * tokens, tokens), 0)
    column = lax.broadcasted_iota(jnp.int32, (heads * tokens, tokens), 1)
    weights = softmax_weights(queries, keys_in, row % 4 == column % 4)
    out = mm(side_by_side(weights.astype(BF)), stack_heads(values_in)).astype(BF)
    grads = attend_back(queries, keys_in, values_in, grad_out, weights)
    wire_ref[...] = to_wire(list(grads) + [out])


def temporal_return(arrived_ref, proj_ref, partial_ref, heads_ref):
    *grads, heads = from_wire(arrived_ref[...])
    heads_ref[...] = heads
    total = mm_rt(grads[0], proj_ref[0]) + mm_rt(grads[1], proj_ref[1])
    partial_ref[...] = (total + mm_rt(grads[2], proj_ref[2])).astype(BF)


def mix_temporal(heads_ref, out_ref, mixed_ref):
    mixed_ref[...] = mm_rt(heads_ref[...], out_ref[...]).astype(BF)


def middle_back(
    place_ref, cot_ref, middle_ref, mod_ref, mine_ref, other_ref, grad_ref, scaled_ref,
    b0, b1, b2, b3, held_ref,
):
    incoming = mine_ref[...].astype(F32) + other_ref[...].astype(F32)
    grad = cot_ref[...].astype(F32) + norm_back(middle_ref[...], mod_ref[4:5], incoming)
    grad_ref[...] = grad
    scaled = (mod_ref[2:3] * grad).astype(BF)
    scaled_ref[...] = scaled
    split_columns(scaled, place_ref[0], held_ref, (b0, b1, b2, b3))


def spatial_back(scaled_ref, packed_ref, weights_ref, out_ref, proj_ref, partial_ref):
    grad_heads = mm(scaled_ref[...], out_ref[...]).astype(BF)
    grads = attend_back(
        packed_ref[0], packed_ref[1], packed_ref[2], grad_heads, weights_ref[...]
    )
    total = mm_rt(grads[0], proj_ref[0]) + mm_rt(grads[1], proj_ref[1])
    partial_ref[...] = (total + mm_rt(grads[2], proj_ref[2])).astype(BF)


def latent_step(x_ref, mod_ref, grad_ref, mine_ref, other_ref, latent_ref):
    incoming = mine_ref[...].astype(F32) + other_ref[...].astype(F32)
    latent_ref[...] = grad_ref[...] + norm_back(x_ref[...].astype(F32), mod_ref[1:2], incoming)


def output_step(middle_ref, mod_ref, mine_ref, other_ref, block_ref):
    mixed = mine_ref[...].astype(F32) + other_ref[...].astype(F32)
    block_ref[...] = (middle_ref[...] + mod_ref[5:6] * mixed).astype(BF)


def weight_products(*refs):
    wire_ref = refs[-1]
    totals = []
    for which in range(2):
        base = which * 2 * DP
        total = mm_lt(refs[base][...], refs[base + DP][...])
        for i in range(1, DP):
            total = total + mm_lt(refs[base + i][...], refs[base + DP + i][...])
        totals.append(total.astype(BF))
    rows = totals[0].shape[0]
    part = rows // SEQ
    shape = (SEQ * ROWS, rows)
    row = lax.broadcasted_iota(jnp.int32, shape, 0)
    column = lax.broadcasted_iota(jnp.int32, (1, rows), 1)
    held = ROWS * (column // part) + column % part
    first = (row == held).astype(F32).astype(BF)
    second = (row == held + part).astype(F32).astype(BF)
    wire_ref[...] = (mm(first, totals[0]) + mm(second, totals[1])).astype(BF)


def weight_sums(arrived_ref, spatial_ref, temporal_ref):
    part = spatial_ref.shape[0]
    shape = (16, SEQ * ROWS)
    row = lax.broadcasted_iota(jnp.int32, shape, 0)
    column = lax.broadcasted_iota(jnp.int32, shape, 1) % ROWS
    arrived = arrived_ref[...]
    for start, ref in ((0, spatial_ref), (part, temporal_ref)):
        take = (column == row + start).astype(F32).astype(BF)
        ref[...] = mm(take, arrived)[:part]


def call(body, outs, *operands, scalars=0, scratch=(), flops=0):
    specs = [pl.BlockSpec(memory_space=pltpu.SMEM)] * scalars
    specs += [pl.BlockSpec(memory_space=pltpu.VMEM)] * (len(operands) - scalars)
    shapes = [jax.ShapeDtypeStruct(shape, dtype) for shape, dtype in outs]
    moved = sum(x.size * x.dtype.itemsize for x in [*operands, *shapes])
    single = len(shapes) == 1
    return pl.pallas_call(
        body,
        out_shape=shapes[0] if single else shapes,
        in_specs=specs,
        out_specs=specs[-1] if single else [specs[-1]] * len(shapes),
        scratch_shapes=list(scratch),
        cost_estimate=pl.CostEstimate(flops=flops, bytes_accessed=moved, transcendentals=0),
        compiler_params=pltpu.CompilerParams(vmem_limit_bytes=40 * 1024 * 1024),
    )(*operands)


def swap_pair(array):
    return lax.ppermute(array, "tensor", PAIR)


def swap_dp(array, mask):
    return lax.ppermute(array, "dp", [(i, i ^ mask) for i in range(DP)])


def all_to_all(array):
    rows, width = array.shape
    cut = array.reshape(SEQ, rows // SEQ, width)
    moved = lax.all_to_all(cut, "seq", split_axis=0, concat_axis=0, tiled=True)
    return moved.reshape(rows, width)


def per_device(
    latents, modulation, cotangent, proj_spatial, out_spatial, proj_temporal, out_temporal
):
    tokens, width = latents.shape[-2:]
    local = out_spatial.shape[1]
    heads = local // HEAD_DIM
    x = latents.reshape(tokens, width)
    cot = cotangent.reshape(tokens, width)
    mod = modulation.reshape(-1, width)
    proj_s = proj_spatial.transpose(1, 0, 2)
    proj_t = proj_temporal.transpose(1, 0, 2)
    place = lax.axis_index("dp").astype(jnp.int32).reshape(1)
    wide = ((tokens, width), BF)
    narrow = ((tokens, local), BF)
    full = ((tokens, width), F32)
    block = ((tokens, width // DP), BF)
    wire = ((4 * tokens, local), BF)
    held = pltpu.VMEM((DP, tokens, width // DP), BF)
    product = 2 * tokens * width * local
    attention = 4 * heads * tokens * tokens * local

    packed_s, weights_s, heads_s, mixed_s = call(
        spatial_forward,
        [((3, tokens, local), BF), ((heads * tokens, tokens), F32), narrow, wide],
        x, mod, proj_s, out_spatial, flops=4 * product + attention,
    )
    mixed_other = swap_pair(mixed_s)
    grad_heads_t, *blocks_t = call(
        upstream_start, [narrow] + [block] * DP,
        place, cot, mod, out_temporal, scalars=1, scratch=[held], flops=product,
    )
    middle, wire_out = call(
        middle_step, [full, wire],
        x, mod, mixed_s, mixed_other, proj_t, grad_heads_t, flops=4 * product,
    )
    arrived = all_to_all(wire_out)
    heads_all_s = [heads_s] + [swap_dp(heads_s, i) for i in range(1, DP)]
    blocks_t = blocks_t[:1] + [swap_dp(blocks_t[i], i) for i in range(1, DP)]
    wire_back = call(temporal_step, [wire], arrived, flops=6 * attention)
    returned = all_to_all(wire_back)
    partial_t, heads_t = call(temporal_return, [wide, narrow], returned, proj_t, flops=4 * product)
    partial_other = swap_pair(partial_t)
    mixed_t = call(mix_temporal, [wide], heads_t, out_temporal, flops=product)
    heads_all_t = [heads_t] + [swap_dp(heads_t, i) for i in range(1, DP)]
    mixed_t_other = swap_pair(mixed_t)
    grad_middle, scaled_s, *blocks_s = call(
        middle_back, [full, wide] + [block] * DP,
        place, cot, middle, mod, partial_t, partial_other, scalars=1, scratch=[held],
    )
    blocks_s = blocks_s[:1] + [swap_dp(blocks_s[i], i) for i in range(1, DP)]
    partial_s = call(
        spatial_back, [wide],
        scaled_s, packed_s, weights_s, out_spatial, proj_s, flops=4 * product + 5 * attention,
    )
    partial_s_other = swap_pair(partial_s)
    sums_out = call(
        weight_products, [((SEQ * ROWS, local), BF)],
        *blocks_s, *heads_all_s, *blocks_t, *heads_all_t, flops=4 * product,
    )
    sums_in = all_to_all(sums_out)
    block_output = call(output_step, [wide], middle, mod, mixed_t, mixed_t_other)
    latent_grad = call(latent_step, [full], x, mod, grad_middle, partial_s, partial_s_other)
    part = ((width // DP // SEQ, local), F32)
    grad_out_s, grad_out_t = call(weight_sums, [part, part], sums_in)
    return (
        block_output.reshape(latents.shape),
        latent_grad.reshape(latents.shape),
        grad_out_s,
        grad_out_t,
    )


def solution(mesh):
    placed = (
        P("dp", "seq", None, None),
        P("dp", None, None),
        P("dp", "seq", None, None),
        P(None, None, "tensor"),
        P(None, "tensor"),
        P(None, None, "tensor"),
        P(None, "tensor"),
    )
    return jax.shard_map(
        per_device,
        mesh=mesh,
        in_specs=placed,
        out_specs=(
            P("dp", "seq", None, None),
            P("dp", "seq", None, None),
            P(("dp", "seq"), "tensor"),
            P(("dp", "seq"), "tensor"),
        ),
        check_vma=False,
    )
```

```python
import functools

import jax
import jax.numpy as jnp
from jax import lax
from jax.experimental import pallas as pl
from jax.experimental.pallas import tpu as pltpu
from jax.sharding import PartitionSpec as P

HEAD_DIM = 72
NORM_EPS = 1e-06
PAIR = ((0, 1), (1, 0))
DP = 4
SEQ = 32
BF = jnp.bfloat16
F32 = jnp.float32
ROWS = 24
X_RING = 4
Z_RING = 8
X_GROUPS = tuple(tuple(z + Z_RING * x for x in range(X_RING)) for z in range(Z_RING))
Z_GROUPS = tuple(tuple(z + Z_RING * x for z in range(Z_RING)) for x in range(X_RING))


def mm(left, right):
    return jnp.dot(left, right, preferred_element_type=F32)


def mm_rt(left, right):
    return lax.dot_general(left, right, (((1,), (1,)), ((), ())), preferred_element_type=F32)


def mm_lt(left, right):
    return lax.dot_general(left, right, (((0,), (0,)), ((), ())), preferred_element_type=F32)


def normalise(values):
    average = jnp.mean(values, axis=-1, keepdims=True)
    centred = values - average
    inverse = lax.rsqrt(jnp.mean(centred * centred, axis=-1, keepdims=True) + NORM_EPS)
    return centred * inverse, inverse


def norm_back(values, scale_row, incoming):
    unit, inverse = normalise(values)
    scaled = incoming * (1.0 + scale_row)
    mean_plain = jnp.mean(scaled, axis=-1, keepdims=True)
    mean_unit = jnp.mean(scaled * unit, axis=-1, keepdims=True)
    return inverse * (scaled - mean_plain - unit * mean_unit)


def stack_heads(values):
    width = values.shape[1]
    owner = lax.broadcasted_iota(jnp.int32, (1, width), 1) // HEAD_DIM
    parts = [values * (owner == head).astype(F32).astype(BF) for head in range(width // HEAD_DIM)]
    return jnp.concatenate(parts, axis=0)


def side_by_side(stacked):
    tokens = stacked.shape[1]
    heads = stacked.shape[0] // tokens
    return jnp.concatenate([stacked[h * tokens : (h + 1) * tokens] for h in range(heads)], axis=1)


def softmax_weights(queries, keys_in, same=None):
    scores = mm_rt(stack_heads(queries), keys_in) * HEAD_DIM**-0.5
    if same is not None:
        scores = jnp.where(same, scores, -1e30)
    raised = jnp.exp(scores - jnp.max(scores, axis=-1, keepdims=True))
    return raised / jnp.sum(raised, axis=-1, keepdims=True)


def attend_back(queries, keys_in, values_in, grad_out, weights):
    grad_stacked = stack_heads(grad_out)
    grad_weights = mm_rt(grad_stacked, values_in)
    inner_sum = jnp.sum(grad_weights * weights, axis=-1, keepdims=True)
    grad_scores = (weights * (grad_weights - inner_sum) * HEAD_DIM**-0.5).astype(BF)
    grad_queries = mm(side_by_side(grad_scores), stack_heads(keys_in)).astype(BF)
    grad_keys = mm_lt(grad_scores, stack_heads(queries)).astype(BF)
    grad_values = mm_lt(weights.astype(BF), grad_stacked).astype(BF)
    return grad_queries, grad_keys, grad_values


def wire_row(index, tokens):
    part, token = index // tokens, index % tokens
    return 16 * (token // 4) + 4 * part + token % 4


def to_wire(parts):
    tokens = parts[0].shape[0]
    rows = 4 * tokens
    held = wire_row(lax.broadcasted_iota(jnp.int32, (1, rows), 1), tokens)
    place = lax.broadcasted_iota(jnp.int32, (rows, rows), 0) == held
    return mm(place.astype(F32).astype(BF), jnp.concatenate(parts, axis=0)).astype(BF)


def from_wire(rows_in):
    rows = rows_in.shape[0]
    tokens = rows // 4
    held = wire_row(lax.broadcasted_iota(jnp.int32, (rows, 1), 0), tokens)
    place = lax.broadcasted_iota(jnp.int32, (rows, rows), 1) == held
    full = mm(place.astype(F32).astype(BF), rows_in).astype(BF)
    return [full[i * tokens : (i + 1) * tokens] for i in range(4)]


def spatial_forward(
    x_ref, mod_ref, proj_hbm, out_hbm, packed_ref, weights_ref, heads_ref, mixed_ref,
    proj_ref, out_ref, sems,
):
    copies = [pltpu.make_async_copy(proj_hbm.at[i], proj_ref.at[i], sems.at[i]) for i in range(3)]
    copies.append(pltpu.make_async_copy(out_hbm, out_ref, sems.at[3]))
    for copy in copies:
        copy.start()
    unit, _ = normalise(x_ref[...].astype(F32))
    normed = (unit * (1.0 + mod_ref[1]) + mod_ref[0]).astype(BF)
    parts = []
    for i in range(3):
        copies[i].wait()
        parts.append(mm_rt(normed, proj_ref[i]).astype(BF))
        packed_ref[i] = parts[i]
    queries, keys_in, values_in = parts
    weights = softmax_weights(queries, keys_in)
    weights_ref[...] = weights
    heads = mm(side_by_side(weights.astype(BF)), stack_heads(values_in)).astype(BF)
    heads_ref[...] = heads
    copies[3].wait()
    mixed_ref[...] = mm(heads, out_ref[...]).astype(BF)


def split_columns(scaled, place, held_ref, block_refs):
    wide = scaled.shape[1] // DP
    for i in range(DP):
        held_ref[i] = scaled[:, i * wide : (i + 1) * wide]
    for i in range(DP):
        block_refs[i][:, block_refs[i].shape[1] - wide :] = held_ref[place ^ i]


def upstream_start(
    place_ref, cot_ref, mod_ref, out_ref, heads_ref, grad_ref, b0, b1, b2, b3, held_ref
):
    scaled = (mod_ref[5] * cot_ref[...].astype(F32)).astype(BF)
    grad_ref[...] = mm_rt(scaled, out_ref[...]).astype(BF)
    split_columns(scaled, place_ref[0], held_ref, (b0, b1, b2, b3))
    local = heads_ref.shape[1]
    for ref in (b1, b2, b3):
        ref[:, :local] = heads_ref[...]


def middle_step(x_ref, mod_ref, mine_ref, other_ref, proj_ref, grad_ref, middle_ref, wire_ref):
    mixed = mine_ref[...].astype(F32) + other_ref[...].astype(F32)
    middle = x_ref[...].astype(F32) + mod_ref[2] * mixed
    middle_ref[...] = middle
    unit, _ = normalise(middle)
    normed = (unit * (1.0 + mod_ref[4]) + mod_ref[3]).astype(BF)
    parts = [mm_rt(normed, proj_ref[i]).astype(BF) for i in range(3)]
    wire_ref[...] = to_wire(parts + [grad_ref[...]])


def temporal_step(arrived_ref, wire_ref):
    queries, keys_in, values_in, grad_out = from_wire(arrived_ref[...])
    tokens = queries.shape[0]
    heads = queries.shape[1] // HEAD_DIM
    row = lax.broadcasted_iota(jnp.int32, (heads * tokens, tokens), 0)
    column = lax.broadcasted_iota(jnp.int32, (heads * tokens, tokens), 1)
    weights = softmax_weights(queries, keys_in, row % 4 == column % 4)
    out = mm(side_by_side(weights.astype(BF)), stack_heads(values_in)).astype(BF)
    grads = attend_back(queries, keys_in, values_in, grad_out, weights)
    wire_ref[...] = to_wire(list(grads) + [out])


def temporal_return(arrived_ref, proj_ref, partial_ref, heads_ref):
    *grads, heads = from_wire(arrived_ref[...])
    heads_ref[...] = heads
    total = mm(grads[0], proj_ref[0]) + mm(grads[1], proj_ref[1])
    partial_ref[...] = (total + mm(grads[2], proj_ref[2])).astype(BF)


def mix_temporal(heads_ref, out_ref, mixed_ref):
    mixed_ref[...] = mm(heads_ref[...], out_ref[...]).astype(BF)


def middle_back(
    place_ref, cot_ref, middle_ref, mod_ref, mine_ref, other_ref, grad_ref, scaled_ref,
    b0, b1, b2, b3, held_ref,
):
    incoming = mine_ref[...].astype(F32) + other_ref[...].astype(F32)
    grad = cot_ref[...].astype(F32) + norm_back(middle_ref[...], mod_ref[4], incoming)
    grad_ref[...] = grad
    scaled = (mod_ref[2] * grad).astype(BF)
    scaled_ref[...] = scaled
    split_columns(scaled, place_ref[0], held_ref, (b0, b1, b2, b3))


def spatial_back(
    scaled_ref, packed_ref, weights_ref, out_ref, proj_hbm, partial_ref, proj_ref, sem
):
    copy = pltpu.make_async_copy(proj_hbm, proj_ref, sem)
    copy.start()
    grad_heads = mm_rt(scaled_ref[...], out_ref[...]).astype(BF)
    grads = attend_back(
        packed_ref[0], packed_ref[1], packed_ref[2], grad_heads, weights_ref[...]
    )
    copy.wait()
    total = mm(grads[0], proj_ref[0]) + mm(grads[1], proj_ref[1])
    partial_ref[...] = (total + mm(grads[2], proj_ref[2])).astype(BF)


def latent_step(x_ref, mod_ref, grad_ref, mine_ref, other_ref, latent_ref):
    incoming = mine_ref[...].astype(F32) + other_ref[...].astype(F32)
    latent_ref[...] = grad_ref[...] + norm_back(x_ref[...].astype(F32), mod_ref[1], incoming)


def output_step(middle_ref, mod_ref, mine_ref, other_ref, block_ref):
    mixed = mine_ref[...].astype(F32) + other_ref[...].astype(F32)
    block_ref[...] = (middle_ref[...] + mod_ref[5] * mixed).astype(BF)


def weight_products(*refs):
    wire_ref = refs[-1]
    own_s, *near_s = refs[:DP]
    own_t, heads_s, heads_t = refs[DP : DP + 3]
    near_t = refs[DP + 3 : 2 * DP + 2]
    heads_near = refs[2 * DP + 2 : 3 * DP + 1]
    local = heads_s.shape[1]
    spatial = mm_lt(own_s[...], heads_s[...])
    temporal = mm_lt(own_t[...], heads_t[...])
    for i in range(DP - 1):
        spatial = spatial + mm_lt(near_s[i][...], near_t[i][:, :local])
        temporal = temporal + mm_lt(near_t[i][:, local:], heads_near[i][...])
    cut = spatial.shape[0] // X_RING
    for i in range(X_RING):
        rows = slice(i * cut, (i + 1) * cut)
        wire_ref[i] = jnp.concatenate([spatial[rows], temporal[rows]], axis=0).astype(BF)


def add_sources(arrived_ref):
    total = arrived_ref[0].astype(F32)
    for i in range(1, arrived_ref.shape[0]):
        total = total + arrived_ref[i].astype(F32)
    return total


def weight_halfway(arrived_ref, wire_ref):
    total = add_sources(arrived_ref).astype(BF)
    rows = total.shape[0]
    part = rows // 2 // Z_RING
    index = lax.broadcasted_iota(jnp.int32, (1, rows), 1)
    which, index = index // (rows // 2), index % (rows // 2)
    held = ROWS * (index // part) + part * which + index % part
    place = lax.broadcasted_iota(jnp.int32, (Z_RING * ROWS, rows), 0) == held
    wire_ref[...] = mm(place.astype(F32).astype(BF), total).astype(BF).reshape(wire_ref.shape)


def weight_sums(arrived_ref, spatial_ref, temporal_ref):
    part = spatial_ref.shape[0]
    total = add_sources(arrived_ref)
    spatial_ref[...] = total[:part]
    temporal_ref[...] = total[part : 2 * part]


def call(body, outs, *operands, scalars=0, apart=(), scratch=(), flops=0, vmem=40):
    specs = [pl.BlockSpec(memory_space=pltpu.SMEM)] * scalars
    specs += [pl.BlockSpec(memory_space=pltpu.VMEM)] * (len(operands) - scalars)
    whole = pl.BlockSpec(memory_space=pltpu.VMEM)
    for i in apart:
        specs[i] = pl.BlockSpec(memory_space=pl.ANY)
    shapes = [jax.ShapeDtypeStruct(shape, dtype) for shape, dtype in outs]
    moved = sum(x.size * x.dtype.itemsize for x in [*operands, *shapes])
    single = len(shapes) == 1
    return pl.pallas_call(
        body,
        out_shape=shapes[0] if single else shapes,
        in_specs=specs,
        out_specs=whole if single else [whole] * len(shapes),
        scratch_shapes=list(scratch),
        cost_estimate=pl.CostEstimate(flops=flops, bytes_accessed=moved, transcendentals=0),
        compiler_params=pltpu.CompilerParams(vmem_limit_bytes=vmem * 1024 * 1024),
    )(*operands)


def swap_pair(array):
    return lax.ppermute(array, "tensor", PAIR)


def swap_dp(array, mask):
    return lax.ppermute(array, "dp", [(i, i ^ mask) for i in range(DP)])


def all_to_all(array):
    rows, width = array.shape
    cut = array.reshape(SEQ, rows // SEQ, width)
    moved = lax.all_to_all(cut, "seq", split_axis=0, concat_axis=0, tiled=True)
    return moved.reshape(rows, width)


def group_all_to_all(array, groups):
    return lax.all_to_all(
        array, "seq", split_axis=0, concat_axis=0, tiled=True, axis_index_groups=groups
    )


def per_device(
    latents, modulation, cotangent, proj_spatial, out_spatial, proj_temporal, out_temporal
):
    tokens, width = latents.shape[-2:]
    local = out_spatial.shape[1]
    heads = local // HEAD_DIM
    x = latents.reshape(tokens, width)
    cot = cotangent.reshape(tokens, width)
    mod = modulation.transpose(1, 0, 2)
    proj_s = proj_spatial.transpose(1, 2, 0)
    proj_t = proj_temporal.transpose(1, 2, 0)
    out_s = out_spatial.T
    out_t = out_temporal.T
    place = lax.axis_index("dp").astype(jnp.int32).reshape(1)
    wide = ((tokens, width), BF)
    narrow = ((tokens, local), BF)
    full = ((tokens, width), F32)
    block = ((tokens, width // DP), BF)
    wire = ((4 * tokens, local), BF)
    held = pltpu.VMEM((DP, tokens, width // DP), BF)
    product = 2 * tokens * width * local
    attention = 4 * heads * tokens * tokens * local

    packed_s, weights_s, heads_s, mixed_s = call(
        spatial_forward,
        [((3, tokens, local), BF), ((heads * tokens, tokens), F32), narrow, wide],
        x, mod, proj_s, out_s, apart=(2, 3), flops=4 * product + attention, vmem=60,
        scratch=[
            pltpu.VMEM(proj_s.shape, BF),
            pltpu.VMEM(out_s.shape, BF),
            pltpu.SemaphoreType.DMA((4,)),
        ],
    )
    mixed_other = swap_pair(mixed_s)
    bundle = ((tokens, local + width // DP), BF)
    grad_heads_t, own_t, *bundles = call(
        upstream_start, [narrow, block] + [bundle] * (DP - 1),
        place, cot, mod, out_t, heads_s, scalars=1, scratch=[held], flops=product,
    )
    middle, wire_out = call(
        middle_step, [full, wire],
        x, mod, mixed_s, mixed_other, proj_t, grad_heads_t, flops=4 * product,
    )
    near_t = [swap_dp(bundles[i], i + 1) for i in range(DP - 1)]
    arrived = all_to_all(wire_out)
    arrived, *near_t = lax.optimization_barrier((arrived, *near_t))
    wire_back = call(temporal_step, [wire], arrived, flops=6 * attention)
    returned = all_to_all(wire_back)
    partial_t, heads_t = call(temporal_return, [wide, narrow], returned, proj_t, flops=4 * product)
    partial_other = swap_pair(partial_t)
    heads_near = [swap_dp(heads_t, i) for i in range(1, DP)]
    grad_middle, scaled_s, *blocks_s = call(
        middle_back, [full, wide] + [block] * DP,
        place, cot, middle, mod, partial_t, partial_other, scalars=1, scratch=[held],
    )
    blocks_s = blocks_s[:1] + [swap_dp(blocks_s[i], i) for i in range(1, DP)]
    partial_s = call(
        spatial_back, [wide],
        scaled_s, packed_s, weights_s, out_s, proj_s, apart=(4,),
        scratch=[pltpu.VMEM(proj_s.shape, BF), pltpu.SemaphoreType.DMA],
        flops=4 * product + 5 * attention,
    )
    partial_s_other = swap_pair(partial_s)
    cut = 2 * width // DP // X_RING
    sums_out = call(
        weight_products, [((X_RING, cut, local), BF)],
        *blocks_s, own_t, heads_s, heads_t, *near_t, *heads_near, flops=4 * product,
    )
    sums_half = group_all_to_all(sums_out, X_GROUPS)
    sums_half = call(weight_halfway, [((Z_RING, ROWS, local), BF)], sums_half)
    sums_in = group_all_to_all(sums_half, Z_GROUPS)
    heads_late, partial_s_other = lax.optimization_barrier((heads_t, partial_s_other))
    mixed_t = call(mix_temporal, [wide], heads_late, out_t, flops=product)
    mixed_t_other = swap_pair(mixed_t)
    block_output = call(output_step, [wide], middle, mod, mixed_t, mixed_t_other)
    latent_grad = call(latent_step, [full], x, mod, grad_middle, partial_s, partial_s_other)
    part = ((width // DP // SEQ, local), F32)
    grad_out_s, grad_out_t = call(weight_sums, [part, part], sums_in)
    return (
        block_output.reshape(latents.shape),
        latent_grad.reshape(latents.shape),
        grad_out_s,
        grad_out_t,
    )


def solution(mesh):
    placed = (
        P("dp", "seq", None, None),
        P("dp", None, None),
        P("dp", "seq", None, None),
        P(None, None, "tensor"),
        P(None, "tensor"),
        P(None, None, "tensor"),
        P(None, "tensor"),
    )
    return jax.shard_map(
        per_device,
        mesh=mesh,
        in_specs=placed,
        out_specs=(
            P("dp", "seq", None, None),
            P("dp", "seq", None, None),
            P(("dp", "seq"), "tensor"),
            P(("dp", "seq"), "tensor"),
        ),
        check_vma=False,
    )
```

```python
import functools

import jax
import jax.numpy as jnp
from jax import lax
from jax.experimental import pallas as pl
from jax.experimental.pallas import tpu as pltpu
from jax.sharding import PartitionSpec as P

HEAD_DIM = 72
NORM_EPS = 1e-06
PAIR = ((0, 1), (1, 0))
DP = 4
SEQ = 32
BF = jnp.bfloat16
F32 = jnp.float32
ROWS = 24
X_RING = 4
Z_RING = 8
Z_GROUPS = tuple(tuple(z + Z_RING * x for z in range(Z_RING)) for x in range(X_RING))


def mm(left, right):
    return jnp.dot(left, right, preferred_element_type=F32)


def mm_rt(left, right):
    return lax.dot_general(left, right, (((1,), (1,)), ((), ())), preferred_element_type=F32)


def mm_lt(left, right):
    return lax.dot_general(left, right, (((0,), (0,)), ((), ())), preferred_element_type=F32)


def normalise(values):
    average = jnp.mean(values, axis=-1, keepdims=True)
    centred = values - average
    inverse = lax.rsqrt(jnp.mean(centred * centred, axis=-1, keepdims=True) + NORM_EPS)
    return centred * inverse, inverse


def norm_back(values, scale_row, incoming):
    unit, inverse = normalise(values)
    scaled = incoming * (1.0 + scale_row)
    mean_plain = jnp.mean(scaled, axis=-1, keepdims=True)
    mean_unit = jnp.mean(scaled * unit, axis=-1, keepdims=True)
    return inverse * (scaled - mean_plain - unit * mean_unit)


def stack_heads(values):
    width = values.shape[1]
    owner = lax.broadcasted_iota(jnp.int32, (1, width), 1) // HEAD_DIM
    parts = [values * (owner == head).astype(F32).astype(BF) for head in range(width // HEAD_DIM)]
    return jnp.concatenate(parts, axis=0)


def side_by_side(stacked):
    tokens = stacked.shape[1]
    heads = stacked.shape[0] // tokens
    return jnp.concatenate([stacked[h * tokens : (h + 1) * tokens] for h in range(heads)], axis=1)


def softmax_weights(queries, keys_in, same=None):
    scores = mm_rt(stack_heads(queries), keys_in) * HEAD_DIM**-0.5
    if same is not None:
        scores = jnp.where(same, scores, -1e30)
    raised = jnp.exp(scores - jnp.max(scores, axis=-1, keepdims=True))
    return raised / jnp.sum(raised, axis=-1, keepdims=True)


def attend_back(queries, keys_in, values_in, grad_out, weights):
    grad_stacked = stack_heads(grad_out)
    grad_weights = mm_rt(grad_stacked, values_in)
    inner_sum = jnp.sum(grad_weights * weights, axis=-1, keepdims=True)
    grad_scores = (weights * (grad_weights - inner_sum) * HEAD_DIM**-0.5).astype(BF)
    grad_queries = mm(side_by_side(grad_scores), stack_heads(keys_in)).astype(BF)
    grad_keys = mm_lt(grad_scores, stack_heads(queries)).astype(BF)
    grad_values = mm_lt(weights.astype(BF), grad_stacked).astype(BF)
    return grad_queries, grad_keys, grad_values


LANES = 128
QUARTERS = 4


def wire_slots(columns):
    slots = QUARTERS * columns // LANES
    return -(-slots // 8) * 8


def wire_pieces(columns):
    pieces, slot = [], 0
    for start in range(0, columns, LANES):
        wide = min(LANES, columns - start)
        for quarter in range(QUARTERS if wide == LANES else QUARTERS // 2):
            pieces.append((slot, start, wide, quarter))
            slot += 1
    return pieces, slot


def to_wire(arrays, held_ref, wire_ref):
    devices = arrays[0].shape[0] // QUARTERS
    slots = held_ref.shape[0] // devices
    base = 0
    for values in arrays:
        values = values.astype(F32)
        pieces, used = wire_pieces(values.shape[1])
        for slot, start, wide, quarter in pieces:
            part = values[quarter * devices : (quarter + 1) * devices, start : start + wide]
            if wide < LANES:
                later = (quarter + 2) * devices
                other = values[later : later + devices, start : start + wide]
                part = jnp.concatenate([part, other], axis=1)
            held_ref[pl.ds(base + slot, devices, stride=slots), :] = part
        base += used
    for slot in range(base, slots):
        held_ref[pl.ds(slot, devices, stride=slots), :] = jnp.zeros((devices, LANES), F32)
    wire_ref[...] = held_ref[...].astype(BF)


def from_wire(wire_ref, held_ref, widths):
    devices = SEQ
    slots = held_ref.shape[0] // devices
    held_ref[...] = wire_ref[...].astype(F32)
    base = 0
    arrays = []
    for columns in widths:
        pieces, used = wire_pieces(columns)
        tiles = {}
        for slot, start, wide, quarter in pieces:
            part = held_ref[pl.ds(base + slot, devices, stride=slots), :]
            if wide < LANES:
                tiles[start, quarter] = part[:, :wide]
                tiles[start, quarter + 2] = part[:, wide:]
            else:
                tiles[start, quarter] = part
        base += used
        starts = sorted({start for start, _ in tiles})
        columns_of = [
            jnp.concatenate([tiles[start, quarter] for quarter in range(QUARTERS)], axis=0)
            for start in starts
        ]
        arrays.append(jnp.concatenate(columns_of, axis=1))
    return arrays


def spatial_forward(
    x_ref, mod_ref, proj_ref, out_ref, packed_ref, weights_ref, heads_ref, mixed_ref
):
    unit, _ = normalise(x_ref[...].astype(F32))
    normed = (unit * (1.0 + mod_ref[1]) + mod_ref[0]).astype(BF)
    parts = []
    for i in range(3):
        parts.append(mm_rt(normed, proj_ref[i]).astype(BF))
        packed_ref[i] = parts[i]
    queries, keys_in, values_in = parts
    weights = softmax_weights(queries, keys_in)
    weights_ref[...] = weights
    heads = mm(side_by_side(weights.astype(BF)), stack_heads(values_in)).astype(BF)
    heads_ref[...] = heads
    mixed_ref[...] = mm(heads, out_ref[...]).astype(BF)


def split_columns(scaled, place, held_ref):
    piece = scaled.shape[1] // (DP * X_RING)
    for x_low in range(2):
        for core in range(2):
            starts = [
                ((far * 2 + core) * X_RING + x_high * 2 + x_low) * piece
                for far in range(2)
                for x_high in range(2)
            ]
            parts = [scaled[:, start : start + piece] for start in starts]
            held_ref[2 * x_low + core] = jnp.concatenate(parts, axis=1)
    return [held_ref[place ^ i] for i in range(DP)]


def upstream_start(
    place_ref, cot_ref, mod_ref, out_ref, x_ref, proj_ref, grad_ref, b0, b1, b2, b3, held_ref
):
    del x_ref, proj_ref
    scaled = (mod_ref[5] * cot_ref[...].astype(F32)).astype(BF)
    grad_ref[...] = mm_rt(scaled, out_ref[...]).astype(BF)
    for block, ref in zip(split_columns(scaled, place_ref[0], held_ref), (b0, b1, b2, b3)):
        ref[...] = block


def middle_step(
    x_ref, mine_ref, other_ref, mod_ref, grad_ref, proj_ref, wire_ref, middle_ref, held_ref
):
    mixed = mine_ref[...].astype(F32) + other_ref[...].astype(F32)
    middle = x_ref[...].astype(F32) + mod_ref[2] * mixed
    middle_ref[...] = middle
    unit, _ = normalise(middle)
    normed = (unit * (1.0 + mod_ref[4]) + mod_ref[3]).astype(BF)
    parts = [mm_rt(normed, proj_ref[i]).astype(BF) for i in range(3)]
    to_wire(parts + [grad_ref[...]], held_ref, wire_ref)


def temporal_step(arrived_ref, wire_ref, held_ref):
    local = arrived_ref.shape[0] * LANES // (QUARTERS * SEQ) // 4
    parts = from_wire(arrived_ref, held_ref, (local,) * 4)
    queries, keys_in, values_in, grad_out = [part.astype(BF) for part in parts]
    tokens = queries.shape[0]
    frames = tokens // QUARTERS
    stacked = (local // HEAD_DIM * tokens, tokens)
    row = lax.broadcasted_iota(jnp.int32, stacked, 0) % tokens
    column = lax.broadcasted_iota(jnp.int32, stacked, 1)
    weights = softmax_weights(queries, keys_in, row // frames == column // frames)
    out = mm(side_by_side(weights.astype(BF)), stack_heads(values_in)).astype(BF)
    grads = attend_back(queries, keys_in, values_in, grad_out, weights)
    to_wire(list(grads) + [out], held_ref, wire_ref)


def temporal_return(arrived_ref, proj_ref, partial_ref, heads_ref, held_ref):
    local = heads_ref.shape[1]
    parts = from_wire(arrived_ref, held_ref, (local,) * 4)
    *grads, heads = [part.astype(BF) for part in parts]
    heads_ref[...] = heads
    total = mm(grads[0], proj_ref[0]) + mm(grads[1], proj_ref[1])
    partial_ref[...] = (total + mm(grads[2], proj_ref[2])).astype(BF)


def mix_temporal(heads_ref, out_ref, mixed_ref):
    mixed_ref[...] = mm(heads_ref[...], out_ref[...]).astype(BF)


def middle_back(
    place_ref, cot_ref, middle_ref, mod_ref, mine_ref, other_ref, b0, b1, b2, b3, scaled_ref, grad_ref,
    held_ref,
):
    incoming = mine_ref[...].astype(F32) + other_ref[...].astype(F32)
    grad = cot_ref[...].astype(F32) + norm_back(middle_ref[...], mod_ref[4], incoming)
    scaled = (mod_ref[2] * grad).astype(BF)
    for block, ref in zip(split_columns(scaled, place_ref[0], held_ref), (b0, b1, b2, b3)):
        ref[...] = block
    scaled_ref[...] = scaled
    grad_ref[...] = grad


def spatial_back(scaled_ref, packed_ref, weights_ref, out_ref, proj_ref, partial_ref):
    grad_heads = mm_rt(scaled_ref[...], out_ref[...]).astype(BF)
    grads = attend_back(
        packed_ref[0], packed_ref[1], packed_ref[2], grad_heads, weights_ref[...]
    )
    total = mm(grads[0], proj_ref[0]) + mm(grads[1], proj_ref[1])
    partial_ref[...] = (total + mm(grads[2], proj_ref[2])).astype(BF)


def latent_step(x_ref, mod_ref, grad_ref, mine_ref, other_ref, latent_ref):
    incoming = mine_ref[...].astype(F32) + other_ref[...].astype(F32)
    latent_ref[...] = grad_ref[...] + norm_back(x_ref[...].astype(F32), mod_ref[1], incoming)


def output_step(middle_ref, mod_ref, mine_ref, other_ref, block_ref):
    mixed = mine_ref[...].astype(F32) + other_ref[...].astype(F32)
    block_ref[...] = (middle_ref[...] + mod_ref[5] * mixed).astype(BF)


def weight_products(place_ref, *refs):
    out_refs, held_ref = refs[4 * DP : -1], refs[-1]
    spatial, temporal = 0.0, 0.0
    for i in range(DP):
        temporal = temporal + mm_lt(refs[2 * DP + i][...], refs[3 * DP + i][...])
    for i in range(DP):
        spatial = spatial + mm_lt(refs[i][...], refs[DP + i][...])
    cut = spatial.shape[0] // DP
    for i in range(DP):
        rows = slice(i * cut, (i + 1) * cut)
        held_ref[i] = jnp.concatenate([spatial[rows], temporal[rows]], axis=0).astype(BF)
    for i in range(DP):
        out_refs[i][...] = held_ref[place_ref[0] ^ i]


def add_sources(parts):
    total = parts[0].astype(F32)
    for part in parts[1:]:
        total = total + part.astype(F32)
    return total


def weight_halfway(*refs):
    wire_ref = refs[-1]
    total = add_sources([ref[...] for ref in refs[:-1]]).astype(BF)
    rows = total.shape[0]
    part = rows // 2 // Z_RING
    index = lax.broadcasted_iota(jnp.int32, (1, rows), 1)
    which, index = index // (rows // 2), index % (rows // 2)
    held = ROWS * (index // part) + part * which + index % part
    place = lax.broadcasted_iota(jnp.int32, (Z_RING * ROWS, rows), 0) == held
    wire_ref[...] = mm(place.astype(F32).astype(BF), total).astype(BF).reshape(wire_ref.shape)


def weight_sums(arrived_ref, spatial_ref, temporal_ref):
    part = spatial_ref.shape[0]
    total = add_sources([arrived_ref[i] for i in range(arrived_ref.shape[0])])
    spatial_ref[...] = total[:part]
    temporal_ref[...] = total[part : 2 * part]


class Late:
    def __init__(self, source, target, sems):
        self.target = target
        self.shape = target.shape
        parts = self.shape[0] if len(self.shape) == 3 and self.shape[0] == 3 else 0
        self.parts = parts
        if parts:
            self.copies = [
                pltpu.make_async_copy(source.at[i], target.at[i], sems.at[i]) for i in range(parts)
            ]
        else:
            self.copies = [pltpu.make_async_copy(source, target, sems.at[0])]
        self.waiting = [True] * len(self.copies)
        for copy in self.copies:
            copy.start()

    def wait(self, wanted):
        for i in wanted:
            if self.waiting[i]:
                self.copies[i].wait()
                self.waiting[i] = False

    def __getitem__(self, index):
        one = self.parts and isinstance(index, int)
        self.wait([index] if one else range(len(self.copies)))
        return self.target[index]


class Early:
    def __init__(self, source, target, sem):
        self.source = source
        self.shape = source.shape
        self.dtype = source.dtype
        self.copy = pltpu.make_async_copy(source, target, sem)
        self.started = False

    def start(self):
        if not self.started:
            self.copy.start()
            self.started = True

    def __setitem__(self, index, value):
        self.source[index] = value
        if index is Ellipsis:
            self.start()


def call(body, outs, *operands, scalars=0, scratch=(), flops=0, manual=False):
    smem, whole = [pl.BlockSpec(memory_space=space) for space in (pltpu.SMEM, pltpu.VMEM)]
    apart = pl.BlockSpec(memory_space=pl.ANY) if manual else whole
    count = len(operands)
    late = range(scalars, count) if manual else ()
    early = range(len(outs)) if manual else ()
    specs = [smem if i < scalars else apart for i in range(count)]
    shapes = [jax.ShapeDtypeStruct(shape, dtype) for shape, dtype in outs]
    out_specs = [apart] * len(outs)
    moved = sum(x.size * x.dtype.itemsize for x in [*operands, *shapes])
    held = [pltpu.VMEM(operands[i].shape, operands[i].dtype) for i in late]
    held += [pltpu.VMEM(shapes[i].shape, shapes[i].dtype) for i in early]
    sems = [pltpu.SemaphoreType.DMA((3,))] * len(late) + [pltpu.SemaphoreType.DMA] * len(early)
    own = list(scratch)

    def wrapped(*refs):
        refs = list(refs)
        extra = refs[count + len(outs) :]
        buffers, marks = extra[len(own) : len(own) + len(held)], extra[len(own) + len(held) :]
        for n, i in enumerate(late):
            refs[i] = Late(refs[i], buffers[n], marks[n])
        results = []
        for n, i in enumerate(early):
            at = len(late) + n
            refs[count + i] = Early(buffers[at], refs[count + i], marks[at])
            results.append(refs[count + i])
        body(*refs[: count + len(outs)], *extra[: len(own)])
        for result in results:
            result.start()
        for result in results:
            result.copy.wait()

    single = len(shapes) == 1
    return pl.pallas_call(
        wrapped,
        out_shape=shapes[0] if single else shapes,
        in_specs=specs,
        out_specs=out_specs[0] if single else out_specs,
        scratch_shapes=own + held + sems,
        cost_estimate=pl.CostEstimate(flops=flops, bytes_accessed=moved, transcendentals=0),
        compiler_params=pltpu.CompilerParams(vmem_limit_bytes=(60 if manual else 40) * 1024 * 1024),
    )(*operands)


def swap_pair(array):
    return lax.ppermute(array, "tensor", PAIR)


def swap_both(array, dp_mask, seq_mask):
    if not seq_mask:
        return swap_dp(array, dp_mask)
    if not dp_mask:
        return lax.ppermute(array, "seq", [(i, i ^ seq_mask) for i in range(SEQ)])
    mask = dp_mask * SEQ + seq_mask
    return lax.ppermute(array, ("dp", "seq"), [(i, i ^ mask) for i in range(DP * SEQ)])


def swap_near(array, index):
    return swap_both(array, index % 2, Z_RING * (index // 2))


def swap_dp(array, mask):
    return lax.ppermute(array, "dp", [(i, i ^ mask) for i in range(DP)])


def all_to_all(array):
    rows, width = array.shape
    cut = array.reshape(SEQ, rows // SEQ, width)
    moved = lax.all_to_all(cut, "seq", split_axis=0, concat_axis=0, tiled=True)
    return moved.reshape(rows, width)


def group_all_to_all(array, groups):
    return lax.all_to_all(
        array, "seq", split_axis=0, concat_axis=0, tiled=True, axis_index_groups=groups
    )


def per_device(
    latents, modulation, cotangent, proj_spatial, out_spatial, proj_temporal, out_temporal
):
    tokens, width = latents.shape[-2:]
    local = out_spatial.shape[1]
    heads = local // HEAD_DIM
    x = latents.reshape(tokens, width)
    cot = cotangent.reshape(tokens, width)
    mod = modulation.transpose(1, 0, 2)
    proj_s = proj_spatial.transpose(1, 2, 0)
    proj_t = proj_temporal.transpose(1, 2, 0)
    out_s = out_spatial.T
    out_t = out_temporal.T
    dp, seq = lax.axis_index("dp"), lax.axis_index("seq")
    x_low, x_high = seq // Z_RING % 2, seq // Z_RING // 2
    near_place = (2 * x_low + dp % 2).astype(jnp.int32).reshape(1)
    far_place = (2 * (dp // 2) + x_high).astype(jnp.int32).reshape(1)
    wide = ((tokens, width), BF)
    narrow = ((tokens, local), BF)
    full = ((tokens, width), F32)
    block = ((tokens, width // DP), BF)
    blocks_held = pltpu.VMEM((DP, tokens, width // DP), BF)
    slots = wire_slots(4 * local)
    wire = ((SEQ * slots, LANES), BF)
    wire_held = pltpu.VMEM((SEQ * slots, LANES), F32)
    product = 2 * tokens * width * local
    attention = 4 * heads * tokens * tokens * local

    packed_s, weights_s, heads_s, mixed_s = call(
        spatial_forward,
        [((3, tokens, local), BF), ((heads * tokens, tokens), F32), narrow, wide],
        x, mod, proj_s, out_s, manual=True, flops=4 * product + attention,
    )
    mixed_other = swap_pair(mixed_s)
    grad_heads_t, *blocks_t = call(
        upstream_start, [narrow] + [block] * DP,
        near_place, cot, mod, out_t, x, proj_t, scalars=1, scratch=[blocks_held], flops=product,
    )
    heads_x = swap_near(heads_s, 2)
    heads_core = swap_near(heads_s, 1)
    mixed_other, heads_x, heads_core = lax.optimization_barrier((mixed_other, heads_x, heads_core))
    wire_out, middle = call(
        middle_step, [wire, full],
        x, mixed_s, mixed_other, mod, grad_heads_t, proj_t, scratch=[wire_held],
        flops=4 * product,
    )
    heads_s = [heads_s, heads_core, heads_x, swap_near(heads_x, 1)]
    blocks_t = [blocks_t[0]] + [swap_near(blocks_t[i], i) for i in range(1, DP)]
    arrived = all_to_all(wire_out)
    wire_back = call(
        temporal_step, [wire], arrived, scratch=[wire_held], flops=6 * attention
    )
    returned = all_to_all(wire_back)
    returned, heads_s, blocks_t = lax.optimization_barrier((returned, heads_s, blocks_t))
    partial_t, heads_t = call(
        temporal_return, [wide, narrow], returned, proj_t, scratch=[wire_held], flops=4 * product
    )
    partial_other = swap_pair(partial_t)
    heads_near = [swap_near(heads_t, i) for i in range(1, DP)]
    *blocks_s, scaled_s, grad_middle = call(
        middle_back, [block] * DP + [wide, full],
        near_place, cot, middle, mod, partial_t, partial_other, scalars=1, scratch=[blocks_held],
    )
    blocks_s = [blocks_s[0]] + [swap_near(blocks_s[i], i) for i in range(1, DP)]
    partial_s = call(
        spatial_back, [wide],
        scaled_s, packed_s, weights_s, out_s, proj_s, flops=4 * product + 5 * attention,
    )
    partial_s_other = swap_pair(partial_s)
    piece = ((2 * width // DP // X_RING, local), BF)
    sums = call(
        weight_products, [piece] * DP,
        far_place, *blocks_s, *heads_s, *blocks_t, heads_t, *heads_near, scalars=1, manual=True,
        flops=4 * product, scratch=[pltpu.VMEM((DP, *piece[0]), BF)],
    )
    sums = [sums[0]] + [
        swap_both(sums[i], 2 * (i // 2), 2 * Z_RING * (i % 2)) for i in range(1, DP)
    ]
    sums_half = call(weight_halfway, [((Z_RING, ROWS, local), BF)], *sums)
    sums_in = group_all_to_all(sums_half, Z_GROUPS)
    heads_late, partial_s_other = lax.optimization_barrier((heads_t, partial_s_other))
    mixed_t = call(mix_temporal, [wide], heads_late, out_t, flops=product)
    mixed_t_other = swap_pair(mixed_t)
    block_output = call(output_step, [wide], middle, mod, mixed_t, mixed_t_other)
    latent_grad = call(latent_step, [full], x, mod, grad_middle, partial_s, partial_s_other)
    part = ((width // DP // SEQ, local), F32)
    grad_out_s, grad_out_t = call(weight_sums, [part, part], sums_in)
    return (
        block_output.reshape(latents.shape),
        latent_grad.reshape(latents.shape),
        grad_out_s,
        grad_out_t,
    )


def solution(mesh):
    placed = (
        P("dp", "seq", None, None),
        P("dp", None, None),
        P("dp", "seq", None, None),
        P(None, None, "tensor"),
        P(None, "tensor"),
        P(None, None, "tensor"),
        P(None, "tensor"),
    )
    return jax.shard_map(
        per_device,
        mesh=mesh,
        in_specs=placed,
        out_specs=(
            P("dp", "seq", None, None),
            P("dp", "seq", None, None),
            P(("dp", "seq"), "tensor"),
            P(("dp", "seq"), "tensor"),
        ),
        check_vma=False,
    )
```

```python
import functools

import jax
import jax.numpy as jnp
from jax import lax
from jax.experimental import pallas as pl
from jax.experimental.pallas import tpu as pltpu
from jax.sharding import PartitionSpec as P

HEAD_DIM = 72
NORM_EPS = 1e-06
PAIR = ((0, 1), (1, 0))
DP = 4
SEQ = 32
BF = jnp.bfloat16
F32 = jnp.float32
X_RING = 4
Z_RING = 8


def mm(left, right):
    return jnp.dot(left, right, preferred_element_type=F32)


def mm_rt(left, right):
    return lax.dot_general(left, right, (((1,), (1,)), ((), ())), preferred_element_type=F32)


def mm_lt(left, right):
    return lax.dot_general(left, right, (((0,), (0,)), ((), ())), preferred_element_type=F32)


def normalise(values):
    average = jnp.mean(values, axis=-1, keepdims=True)
    centred = values - average
    inverse = lax.rsqrt(jnp.mean(centred * centred, axis=-1, keepdims=True) + NORM_EPS)
    return centred * inverse, inverse


def norm_back(values, scale_row, incoming):
    unit, inverse = normalise(values)
    scaled = incoming * (1.0 + scale_row)
    mean_plain = jnp.mean(scaled, axis=-1, keepdims=True)
    mean_unit = jnp.mean(scaled * unit, axis=-1, keepdims=True)
    return inverse * (scaled - mean_plain - unit * mean_unit)


def stack_heads(values):
    width = values.shape[1]
    owner = lax.broadcasted_iota(jnp.int32, (1, width), 1) // HEAD_DIM
    parts = [values * (owner == head).astype(F32).astype(BF) for head in range(width // HEAD_DIM)]
    return jnp.concatenate(parts, axis=0)


def side_by_side(stacked):
    tokens = stacked.shape[1]
    heads = stacked.shape[0] // tokens
    return jnp.concatenate([stacked[h * tokens : (h + 1) * tokens] for h in range(heads)], axis=1)


def softmax_weights(queries, keys_in, same=None):
    scores = mm_rt(stack_heads(queries), keys_in) * HEAD_DIM**-0.5
    if same is not None:
        scores = jnp.where(same, scores, -1e30)
    raised = jnp.exp(scores - jnp.max(scores, axis=-1, keepdims=True))
    return raised / jnp.sum(raised, axis=-1, keepdims=True)


def attend_back(queries, keys_in, values_in, grad_out, weights):
    grad_stacked = stack_heads(grad_out)
    grad_weights = mm_rt(grad_stacked, values_in)
    inner_sum = jnp.sum(grad_weights * weights, axis=-1, keepdims=True)
    grad_scores = (weights * (grad_weights - inner_sum) * HEAD_DIM**-0.5).astype(BF)
    grad_queries = mm(side_by_side(grad_scores), stack_heads(keys_in)).astype(BF)
    grad_keys = mm_lt(grad_scores, stack_heads(queries)).astype(BF)
    grad_values = mm_lt(weights.astype(BF), grad_stacked).astype(BF)
    return grad_queries, grad_keys, grad_values


FAR_GROUPS = tuple(
    tuple(
        ((2 * far + core) * X_RING + 2 * x_high + x_low) * Z_RING + z
        for far in range(2)
        for x_high in range(2)
        for z in range(Z_RING)
    )
    for core in range(2)
    for x_low in range(2)
)
LANES = 128
QUARTERS = 4


def wire_slots(columns):
    slots = QUARTERS * columns // LANES
    return -(-slots // 8) * 8


def wire_pieces(columns):
    pieces, slot = [], 0
    for start in range(0, columns, LANES):
        wide = min(LANES, columns - start)
        for quarter in range(QUARTERS if wide == LANES else QUARTERS // 2):
            pieces.append((slot, start, wide, quarter))
            slot += 1
    return pieces, slot


def to_wire(arrays, held_ref, wire_ref):
    devices = arrays[0].shape[0] // QUARTERS
    slots = held_ref.shape[0] // devices
    base = 0
    for values in arrays:
        values = values.astype(F32)
        pieces, used = wire_pieces(values.shape[1])
        for slot, start, wide, quarter in pieces:
            part = values[quarter * devices : (quarter + 1) * devices, start : start + wide]
            if wide < LANES:
                later = (quarter + 2) * devices
                other = values[later : later + devices, start : start + wide]
                part = jnp.concatenate([part, other], axis=1)
            held_ref[pl.ds(base + slot, devices, stride=slots), :] = part
        base += used
    for slot in range(base, slots):
        held_ref[pl.ds(slot, devices, stride=slots), :] = jnp.zeros((devices, LANES), F32)
    wire_ref[...] = held_ref[...].astype(BF)


def from_wire(wire_ref, held_ref, widths):
    devices = SEQ
    slots = held_ref.shape[0] // devices
    held_ref[...] = wire_ref[...].astype(F32)
    base = 0
    arrays = []
    for columns in widths:
        pieces, used = wire_pieces(columns)
        tiles = {}
        for slot, start, wide, quarter in pieces:
            part = held_ref[pl.ds(base + slot, devices, stride=slots), :]
            if wide < LANES:
                tiles[start, quarter] = part[:, :wide]
                tiles[start, quarter + 2] = part[:, wide:]
            else:
                tiles[start, quarter] = part
        base += used
        starts = sorted({start for start, _ in tiles})
        columns_of = [
            jnp.concatenate([tiles[start, quarter] for quarter in range(QUARTERS)], axis=0)
            for start in starts
        ]
        arrays.append(jnp.concatenate(columns_of, axis=1))
    return arrays


def spatial_forward(
    x_ref, mod_ref, proj_ref, out_ref, packed_ref, weights_ref, heads_ref, mixed_ref
):
    unit, _ = normalise(x_ref[...].astype(F32))
    normed = (unit * (1.0 + mod_ref[1]) + mod_ref[0]).astype(BF)
    parts = []
    for i in range(3):
        parts.append(mm_rt(normed, proj_ref[i]).astype(BF))
        packed_ref[i] = parts[i]
    queries, keys_in, values_in = parts
    weights = softmax_weights(queries, keys_in)
    weights_ref[...] = weights
    heads = mm(side_by_side(weights.astype(BF)), stack_heads(values_in)).astype(BF)
    heads_ref[...] = heads
    mixed_ref[...] = mm(heads, out_ref[...]).astype(BF)


def split_columns(scaled, place, held_ref):
    piece = scaled.shape[1] // (DP * X_RING)
    for x_low in range(2):
        for core in range(2):
            starts = [
                ((far * 2 + core) * X_RING + x_high * 2 + x_low) * piece
                for far in range(2)
                for x_high in range(2)
            ]
            parts = [scaled[:, start : start + piece] for start in starts]
            held_ref[2 * x_low + core] = jnp.concatenate(parts, axis=1)
    return [held_ref[place ^ i] for i in range(DP)]


def upstream_start(
    place_ref, cot_ref, mod_ref, out_ref, x_ref, proj_ref, grad_ref, b0, b1, b2, b3, held_ref
):
    del x_ref, proj_ref
    scaled = (mod_ref[5] * cot_ref[...].astype(F32)).astype(BF)
    grad_ref[...] = mm_rt(scaled, out_ref[...]).astype(BF)
    for block, ref in zip(split_columns(scaled, place_ref[0], held_ref), (b0, b1, b2, b3)):
        ref[...] = block


def middle_step(
    x_ref, mine_ref, other_ref, mod_ref, grad_ref, proj_ref, wire_ref, middle_ref, held_ref
):
    mixed = mine_ref[...].astype(F32) + other_ref[...].astype(F32)
    middle = x_ref[...].astype(F32) + mod_ref[2] * mixed
    middle_ref[...] = middle
    unit, _ = normalise(middle)
    normed = (unit * (1.0 + mod_ref[4]) + mod_ref[3]).astype(BF)
    parts = [mm_rt(normed, proj_ref[i]).astype(BF) for i in range(3)]
    to_wire(parts + [grad_ref[...]], held_ref, wire_ref)


def temporal_step(arrived_ref, proj_ref, wire_ref, held_ref, back_ref):
    local = arrived_ref.shape[0] * LANES // (QUARTERS * SEQ) // 4
    parts = from_wire(arrived_ref, held_ref, (local,) * 4)
    queries, keys_in, values_in, grad_out = [part.astype(BF) for part in parts]
    tokens = queries.shape[0]
    frames = tokens // QUARTERS
    stacked = (local // HEAD_DIM * tokens, tokens)
    row = lax.broadcasted_iota(jnp.int32, stacked, 0) % tokens
    column = lax.broadcasted_iota(jnp.int32, stacked, 1)
    weights = softmax_weights(queries, keys_in, row // frames == column // frames)
    out = mm(side_by_side(weights.astype(BF)), stack_heads(values_in)).astype(BF)
    grads = attend_back(queries, keys_in, values_in, grad_out, weights)
    total = mm(grads[0], proj_ref[0]) + mm(grads[1], proj_ref[1])
    partial = (total + mm(grads[2], proj_ref[2])).astype(BF)
    to_wire([partial, out], back_ref, wire_ref)


def temporal_return(arrived_ref, partial_ref, heads_ref, held_ref):
    widths = partial_ref.shape[1], heads_ref.shape[1]
    partial, heads = from_wire(arrived_ref, held_ref, widths)
    partial_ref[...] = partial.astype(BF)
    heads_ref[...] = heads.astype(BF)


def mix_temporal(heads_ref, out_ref, mixed_ref):
    mixed_ref[...] = mm(heads_ref[...], out_ref[...]).astype(BF)


def middle_back(
    place_ref, cot_ref, middle_ref, mod_ref, mine_ref, other_ref, b0, b1, b2, b3, scaled_ref, grad_ref,
    held_ref,
):
    incoming = mine_ref[...].astype(F32) + other_ref[...].astype(F32)
    grad = cot_ref[...].astype(F32) + norm_back(middle_ref[...], mod_ref[4], incoming)
    scaled = (mod_ref[2] * grad).astype(BF)
    for block, ref in zip(split_columns(scaled, place_ref[0], held_ref), (b0, b1, b2, b3)):
        ref[...] = block
    scaled_ref[...] = scaled
    grad_ref[...] = grad


def spatial_back(scaled_ref, out_ref, packed_ref, weights_ref, proj_ref, partial_ref):
    grad_heads = mm_rt(scaled_ref[...], out_ref[...]).astype(BF)
    grads = attend_back(
        packed_ref[0], packed_ref[1], packed_ref[2], grad_heads, weights_ref[...]
    )
    total = mm(grads[0], proj_ref[0]) + mm(grads[1], proj_ref[1])
    partial_ref[...] = (total + mm(grads[2], proj_ref[2])).astype(BF)


def latent_step(x_ref, mod_ref, grad_ref, mine_ref, other_ref, latent_ref):
    incoming = mine_ref[...].astype(F32) + other_ref[...].astype(F32)
    latent_ref[...] = grad_ref[...] + norm_back(x_ref[...].astype(F32), mod_ref[1], incoming)


def output_step(middle_ref, mod_ref, mine_ref, other_ref, block_ref):
    mixed = mine_ref[...].astype(F32) + other_ref[...].astype(F32)
    block_ref[...] = (middle_ref[...] + mod_ref[5] * mixed).astype(BF)


def product_of(refs):
    total = 0.0
    for i in range(DP):
        total = total + mm_lt(refs[i][...], refs[DP + i][...])
    return total


def temporal_product(*refs):
    refs[-1][...] = product_of(refs[:-1])


def weight_products(*refs):
    temporal_ref, wire_ref, tiles_ref, held_ref = refs[2 * DP :]
    totals = (product_of(refs[: 2 * DP]), temporal_ref[...])
    rows, columns = totals[0].shape
    whole = columns // LANES * LANES
    tiles = [total[:, at : at + LANES] for total in totals for at in range(0, whole, LANES)]
    tiles.append(jnp.concatenate([total[:, whole:] for total in totals], axis=1))
    for i, tile in enumerate(tiles):
        tiles_ref[i * rows : (i + 1) * rows] = tile
    part = rows // SEQ
    slots = held_ref.shape[0] // SEQ
    for slot in range(slots):
        tile, row = slot // part, slot % part
        if tile < len(tiles):
            taken = tiles_ref[pl.ds(tile * rows + row, SEQ, stride=part), :]
        else:
            taken = jnp.zeros((SEQ, LANES), F32)
        held_ref[pl.ds(slot, SEQ, stride=slots), :] = taken
    wire_ref[...] = held_ref[...].astype(BF)


def weight_sums(arrived_ref, spatial_ref, temporal_ref):
    slots = arrived_ref.shape[0] // SEQ
    total = arrived_ref[:slots].astype(F32)
    for i in range(1, SEQ):
        total = total + arrived_ref[i * slots : (i + 1) * slots].astype(F32)
    part, columns = spatial_ref.shape
    whole = columns // LANES * LANES
    at = 0
    for ref in (spatial_ref, temporal_ref):
        for start in range(0, whole, LANES):
            ref[:, start : start + LANES] = total[at : at + part]
            at += part
    spatial_ref[:, whole:] = total[at : at + part, : columns - whole]
    temporal_ref[:, whole:] = total[at : at + part, columns - whole :]


class Late:
    def __init__(self, source, target, sems):
        self.target = target
        self.shape = target.shape
        parts = self.shape[0] if len(self.shape) == 3 and self.shape[0] == 3 else 0
        self.parts = parts
        if parts:
            self.copies = [
                pltpu.make_async_copy(source.at[i], target.at[i], sems.at[i]) for i in range(parts)
            ]
        else:
            self.copies = [pltpu.make_async_copy(source, target, sems.at[0])]
        self.waiting = [True] * len(self.copies)
        for copy in self.copies:
            copy.start()

    def wait(self, wanted):
        for i in wanted:
            if self.waiting[i]:
                self.copies[i].wait()
                self.waiting[i] = False

    def __getitem__(self, index):
        one = self.parts and isinstance(index, int)
        self.wait([index] if one else range(len(self.copies)))
        return self.target[index]


class Early:
    def __init__(self, source, target, sem):
        self.source = source
        self.shape = source.shape
        self.dtype = source.dtype
        self.copy = pltpu.make_async_copy(source, target, sem)
        self.started = False

    def start(self):
        if not self.started:
            self.copy.start()
            self.started = True

    def __setitem__(self, index, value):
        self.source[index] = value
        if index is Ellipsis:
            self.start()


def call(body, outs, *operands, scalars=0, scratch=(), flops=0, manual=False, vmem=0):
    smem, whole = [pl.BlockSpec(memory_space=space) for space in (pltpu.SMEM, pltpu.VMEM)]
    apart = pl.BlockSpec(memory_space=pl.ANY) if manual else whole
    count = len(operands)
    late = range(scalars, count) if manual else ()
    early = range(len(outs)) if manual else ()
    specs = [smem if i < scalars else apart for i in range(count)]
    shapes = [jax.ShapeDtypeStruct(shape, dtype) for shape, dtype in outs]
    out_specs = [apart] * len(outs)
    moved = sum(x.size * x.dtype.itemsize for x in [*operands, *shapes])
    held = [pltpu.VMEM(operands[i].shape, operands[i].dtype) for i in late]
    held += [pltpu.VMEM(shapes[i].shape, shapes[i].dtype) for i in early]
    sems = [pltpu.SemaphoreType.DMA((3,))] * len(late) + [pltpu.SemaphoreType.DMA] * len(early)
    own = list(scratch)

    def wrapped(*refs):
        refs = list(refs)
        extra = refs[count + len(outs) :]
        buffers, marks = extra[len(own) : len(own) + len(held)], extra[len(own) + len(held) :]
        for n, i in enumerate(late):
            refs[i] = Late(refs[i], buffers[n], marks[n])
        results = []
        for n, i in enumerate(early):
            at = len(late) + n
            refs[count + i] = Early(buffers[at], refs[count + i], marks[at])
            results.append(refs[count + i])
        body(*refs[: count + len(outs)], *extra[: len(own)])
        for result in results:
            result.start()
        for result in results:
            result.copy.wait()

    single = len(shapes) == 1
    return pl.pallas_call(
        wrapped,
        out_shape=shapes[0] if single else shapes,
        in_specs=specs,
        out_specs=out_specs[0] if single else out_specs,
        scratch_shapes=own + held + sems,
        cost_estimate=pl.CostEstimate(flops=flops, bytes_accessed=moved, transcendentals=0),
        compiler_params=pltpu.CompilerParams(vmem_limit_bytes=(vmem or (60 if manual else 40)) * 1024 * 1024),
    )(*operands)


def swap_pair(array):
    return lax.ppermute(array, "tensor", PAIR)


def swap_both(array, dp_mask, seq_mask):
    if not seq_mask:
        return swap_dp(array, dp_mask)
    if not dp_mask:
        return lax.ppermute(array, "seq", [(i, i ^ seq_mask) for i in range(SEQ)])
    mask = dp_mask * SEQ + seq_mask
    return lax.ppermute(array, ("dp", "seq"), [(i, i ^ mask) for i in range(DP * SEQ)])


def swap_near(array, index):
    return swap_both(array, index % 2, Z_RING * (index // 2))


def swap_dp(array, mask):
    return lax.ppermute(array, "dp", [(i, i ^ mask) for i in range(DP)])


def all_to_all(array):
    rows, width = array.shape
    cut = array.reshape(SEQ, rows // SEQ, width)
    moved = lax.all_to_all(cut, "seq", split_axis=0, concat_axis=0, tiled=True)
    return moved.reshape(rows, width)


def per_device(
    latents, modulation, cotangent, proj_spatial, out_spatial, proj_temporal, out_temporal
):
    tokens, width = latents.shape[-2:]
    local = out_spatial.shape[1]
    heads = local // HEAD_DIM
    x = latents.reshape(tokens, width)
    cot = cotangent.reshape(tokens, width)
    mod = modulation.transpose(1, 0, 2)
    proj_s = proj_spatial.transpose(1, 2, 0)
    proj_t = proj_temporal.transpose(1, 2, 0)
    out_s = out_spatial.T
    out_t = out_temporal.T
    dp, seq = lax.axis_index("dp"), lax.axis_index("seq")
    x_low = seq // Z_RING % 2
    near_place = (2 * x_low + dp % 2).astype(jnp.int32).reshape(1)
    wide = ((tokens, width), BF)
    narrow = ((tokens, local), BF)
    full = ((tokens, width), F32)
    block = ((tokens, width // DP), BF)
    blocks_held = pltpu.VMEM((DP, tokens, width // DP), BF)
    slots = wire_slots(4 * local)
    wire = ((SEQ * slots, LANES), BF)
    wire_held = pltpu.VMEM((SEQ * slots, LANES), F32)
    slots = wire_slots(width + local)
    back = ((SEQ * slots, LANES), BF)
    back_held = pltpu.VMEM((SEQ * slots, LANES), F32)
    product = 2 * tokens * width * local
    attention = 4 * heads * tokens * tokens * local

    packed_s, weights_s, heads_s, mixed_s = call(
        spatial_forward,
        [((3, tokens, local), BF), ((heads * tokens, tokens), F32), narrow, wide],
        x, mod, proj_s, out_s, manual=True, flops=4 * product + attention,
    )
    mixed_other = swap_pair(mixed_s)
    grad_heads_t, *blocks_t = call(
        upstream_start, [narrow] + [block] * DP,
        near_place, cot, mod, out_t, x, proj_t, scalars=1, scratch=[blocks_held], flops=product,
    )
    heads_x = swap_near(heads_s, 2)
    heads_core = swap_near(heads_s, 1)
    mixed_other, heads_x, heads_core = lax.optimization_barrier((mixed_other, heads_x, heads_core))
    wire_out, middle = call(
        middle_step, [wire, full],
        x, mixed_s, mixed_other, mod, grad_heads_t, proj_t, scratch=[wire_held],
        flops=4 * product,
    )
    heads_s = [heads_s, heads_core, heads_x, swap_near(heads_x, 1)]
    blocks_t = [blocks_t[0]] + [swap_near(blocks_t[i], i) for i in range(1, DP)]
    arrived = all_to_all(wire_out)
    wire_back = call(
        temporal_step, [back], arrived, proj_t, manual=True, vmem=40, scratch=[wire_held, back_held],
        flops=3 * product + 6 * attention,
    )
    returned = all_to_all(wire_back)
    returned, heads_s, blocks_t = lax.optimization_barrier((returned, heads_s, blocks_t))
    partial_t, heads_t = call(
        temporal_return, [wide, narrow], returned, scratch=[back_held]
    )
    partial_other = swap_pair(partial_t)
    heads_near = [swap_near(heads_t, i) for i in range(1, DP)]
    *blocks_s, scaled_s, grad_middle = call(
        middle_back, [block] * DP + [wide, full],
        near_place, cot, middle, mod, partial_t, partial_other, scalars=1, scratch=[blocks_held],
    )
    blocks_s = [blocks_s[0]] + [swap_near(blocks_s[i], i) for i in range(1, DP)]
    partial_s = call(
        spatial_back, [wide],
        scaled_s, out_s, packed_s, weights_s, proj_s, manual=True,
        flops=4 * product + 5 * attention,
    )
    partial_s_other = swap_pair(partial_s)
    temporal_sum = call(
        temporal_product, [((width // DP, local), F32)], *blocks_t, heads_t, *heads_near, manual=True,
        flops=2 * product, vmem=60,
    )
    slots = wire_slots(2 * width // DP // SEQ * local // QUARTERS)
    sums = call(
        weight_products, [((SEQ * slots, LANES), BF)],
        *blocks_s, *heads_s, temporal_sum, manual=True, flops=2 * product, vmem=60,
        scratch=[
            pltpu.VMEM((2 * local // LANES * width // DP, LANES), F32),
            pltpu.VMEM((SEQ * slots, LANES), F32),
        ],
    )
    heads_late, sums = lax.optimization_barrier((heads_t, sums))
    mixed_t = call(mix_temporal, [wide], heads_late, out_t, flops=product)
    mixed_t_other = swap_pair(mixed_t)
    sums = lax.all_to_all(
        sums.reshape(SEQ, slots, LANES), ("dp", "seq"), split_axis=0, concat_axis=0, tiled=True,
        axis_index_groups=FAR_GROUPS,
    ).reshape(SEQ * slots, LANES)
    block_output = call(output_step, [wide], middle, mod, mixed_t, mixed_t_other)
    latent_grad = call(latent_step, [full], x, mod, grad_middle, partial_s, partial_s_other)
    part = ((width // DP // SEQ, local), F32)
    grad_out_s, grad_out_t = call(weight_sums, [part, part], sums)
    return (
        block_output.reshape(latents.shape),
        latent_grad.reshape(latents.shape),
        grad_out_s,
        grad_out_t,
    )


def solution(mesh):
    placed = (
        P("dp", "seq", None, None),
        P("dp", None, None),
        P("dp", "seq", None, None),
        P(None, None, "tensor"),
        P(None, "tensor"),
        P(None, None, "tensor"),
        P(None, "tensor"),
    )
    return jax.shard_map(
        per_device,
        mesh=mesh,
        in_specs=placed,
        out_specs=(
            P("dp", "seq", None, None),
            P("dp", "seq", None, None),
            P(("dp", "seq"), "tensor"),
            P(("dp", "seq"), "tensor"),
        ),
        check_vma=False,
    )
```

```python
import functools

import jax
import jax.numpy as jnp
from jax import lax
from jax.experimental import pallas as pl
from jax.experimental.pallas import tpu as pltpu
from jax.sharding import PartitionSpec as P

HEAD_DIM = 72
NORM_EPS = 1e-06
PAIR = ((0, 1), (1, 0))
DP = 4
SEQ = 32
BF = jnp.bfloat16
F32 = jnp.float32
X_RING = 4
Z_RING = 8


def mm(left, right):
    return jnp.dot(left, right, preferred_element_type=F32)


def mm_rt(left, right):
    return lax.dot_general(left, right, (((1,), (1,)), ((), ())), preferred_element_type=F32)


def mm_lt(left, right):
    return lax.dot_general(left, right, (((0,), (0,)), ((), ())), preferred_element_type=F32)


def normalise(values):
    average = jnp.mean(values, axis=-1, keepdims=True)
    centred = values - average
    inverse = lax.rsqrt(jnp.mean(centred * centred, axis=-1, keepdims=True) + NORM_EPS)
    return centred * inverse, inverse


def norm_back(values, scale_row, incoming):
    unit, inverse = normalise(values)
    scaled = incoming * (1.0 + scale_row)
    mean_plain = jnp.mean(scaled, axis=-1, keepdims=True)
    mean_unit = jnp.mean(scaled * unit, axis=-1, keepdims=True)
    return inverse * (scaled - mean_plain - unit * mean_unit)


def stack_heads(values):
    width = values.shape[1]
    owner = lax.broadcasted_iota(jnp.int32, (1, width), 1) // HEAD_DIM
    parts = [values * (owner == head).astype(F32).astype(BF) for head in range(width // HEAD_DIM)]
    return jnp.concatenate(parts, axis=0)


def side_by_side(stacked):
    tokens = stacked.shape[1]
    heads = stacked.shape[0] // tokens
    return jnp.concatenate([stacked[h * tokens : (h + 1) * tokens] for h in range(heads)], axis=1)


def softmax_weights(queries, keys_in, same=None):
    scores = mm_rt(stack_heads(queries), keys_in) * HEAD_DIM**-0.5
    if same is not None:
        scores = jnp.where(same, scores, -1e30)
    raised = jnp.exp(scores - jnp.max(scores, axis=-1, keepdims=True))
    return raised / jnp.sum(raised, axis=-1, keepdims=True)


def attend_back(queries, keys_in, values_in, grad_out, weights):
    grad_stacked = stack_heads(grad_out)
    grad_weights = mm_rt(grad_stacked, values_in)
    inner_sum = jnp.sum(grad_weights * weights, axis=-1, keepdims=True)
    grad_scores = (weights * (grad_weights - inner_sum) * HEAD_DIM**-0.5).astype(BF)
    grad_queries = mm(side_by_side(grad_scores), stack_heads(keys_in)).astype(BF)
    grad_keys = mm_lt(grad_scores, stack_heads(queries)).astype(BF)
    grad_values = mm_lt(weights.astype(BF), grad_stacked).astype(BF)
    return grad_queries, grad_keys, grad_values


FAR_GROUPS = tuple(
    tuple(
        ((2 * far + core) * X_RING + 2 * x_high + x_low) * Z_RING + z
        for far in range(2)
        for x_high in range(2)
        for z in range(Z_RING)
    )
    for core in range(2)
    for x_low in range(2)
)
LANES = 128
QUARTERS = 4


def wire_slots(columns):
    slots = QUARTERS * columns // LANES
    return -(-slots // 8) * 8


def wire_pieces(columns):
    pieces, slot = [], 0
    for start in range(0, columns, LANES):
        wide = min(LANES, columns - start)
        for quarter in range(QUARTERS if wide == LANES else QUARTERS // 2):
            pieces.append((slot, start, wide, quarter))
            slot += 1
    return pieces, slot


def to_wire(arrays, held_ref, wire_ref):
    devices = arrays[0].shape[0] // QUARTERS
    slots = held_ref.shape[0] // devices
    base = 0
    for values in arrays:
        values = values.astype(F32)
        pieces, used = wire_pieces(values.shape[1])
        for slot, start, wide, quarter in pieces:
            part = values[quarter * devices : (quarter + 1) * devices, start : start + wide]
            if wide < LANES:
                later = (quarter + 2) * devices
                other = values[later : later + devices, start : start + wide]
                part = jnp.concatenate([part, other], axis=1)
            held_ref[pl.ds(base + slot, devices, stride=slots), :] = part
        base += used
    for slot in range(base, slots):
        held_ref[pl.ds(slot, devices, stride=slots), :] = jnp.zeros((devices, LANES), F32)
    wire_ref[...] = held_ref[...].astype(BF)


def from_wire(wire_ref, held_ref, widths):
    devices = SEQ
    slots = held_ref.shape[0] // devices
    held_ref[...] = wire_ref[...].astype(F32)
    base = 0
    arrays = []
    for columns in widths:
        pieces, used = wire_pieces(columns)
        tiles = {}
        for slot, start, wide, quarter in pieces:
            part = held_ref[pl.ds(base + slot, devices, stride=slots), :]
            if wide < LANES:
                tiles[start, quarter] = part[:, :wide]
                tiles[start, quarter + 2] = part[:, wide:]
            else:
                tiles[start, quarter] = part
        base += used
        starts = sorted({start for start, _ in tiles})
        columns_of = [
            jnp.concatenate([tiles[start, quarter] for quarter in range(QUARTERS)], axis=0)
            for start in starts
        ]
        arrays.append(jnp.concatenate(columns_of, axis=1))
    return arrays


def spatial_forward(
    x_ref, mod_ref, proj_ref, out_ref, packed_ref, weights_ref, heads_ref, mixed_ref
):
    unit, _ = normalise(x_ref[...].astype(F32))
    normed = (unit * (1.0 + mod_ref[1]) + mod_ref[0]).astype(BF)
    parts = []
    for i in range(3):
        parts.append(mm_rt(normed, proj_ref[i]).astype(BF))
        packed_ref[i] = parts[i]
    queries, keys_in, values_in = parts
    weights = softmax_weights(queries, keys_in)
    weights_ref[...] = weights
    heads = mm(side_by_side(weights.astype(BF)), stack_heads(values_in)).astype(BF)
    heads_ref[...] = heads
    mixed_ref[...] = mm(heads, out_ref[...]).astype(BF)


def split_columns(scaled, place, held_ref):
    piece = scaled.shape[1] // (DP * X_RING)
    for x_low in range(2):
        for core in range(2):
            starts = [
                ((far * 2 + core) * X_RING + x_high * 2 + x_low) * piece
                for far in range(2)
                for x_high in range(2)
            ]
            parts = [scaled[:, start : start + piece] for start in starts]
            held_ref[2 * x_low + core] = jnp.concatenate(parts, axis=1)
    return [held_ref[place ^ i] for i in range(DP)]


def upstream_start(
    place_ref, cot_ref, mod_ref, out_ref, x_ref, proj_ref, grad_ref, b0, b1, b2, b3, held_ref
):
    del x_ref, proj_ref
    scaled = (mod_ref[5] * cot_ref[...].astype(F32)).astype(BF)
    grad_ref[...] = mm_rt(scaled, out_ref[...]).astype(BF)
    for block, ref in zip(split_columns(scaled, place_ref[0], held_ref), (b0, b1, b2, b3)):
        ref[...] = block


def middle_step(
    x_ref, mine_ref, other_ref, mod_ref, grad_ref, proj_ref, wire_ref, middle_ref, held_ref
):
    mixed = mine_ref[...].astype(F32) + other_ref[...].astype(F32)
    middle = x_ref[...].astype(F32) + mod_ref[2] * mixed
    middle_ref[...] = middle
    unit, _ = normalise(middle)
    normed = (unit * (1.0 + mod_ref[4]) + mod_ref[3]).astype(BF)
    parts = [mm_rt(normed, proj_ref[i]).astype(BF) for i in range(3)]
    to_wire(parts + [grad_ref[...]], held_ref, wire_ref)


def temporal_step(arrived_ref, proj_ref, wire_ref, held_ref, back_ref):
    local = arrived_ref.shape[0] * LANES // (QUARTERS * SEQ) // 4
    parts = from_wire(arrived_ref, held_ref, (local,) * 4)
    queries, keys_in, values_in, grad_out = [part.astype(BF) for part in parts]
    tokens = queries.shape[0]
    frames = tokens // QUARTERS
    stacked = (local // HEAD_DIM * tokens, tokens)
    row = lax.broadcasted_iota(jnp.int32, stacked, 0) % tokens
    column = lax.broadcasted_iota(jnp.int32, stacked, 1)
    weights = softmax_weights(queries, keys_in, row // frames == column // frames)
    out = mm(side_by_side(weights.astype(BF)), stack_heads(values_in)).astype(BF)
    grads = attend_back(queries, keys_in, values_in, grad_out, weights)
    total = mm(grads[0], proj_ref[0]) + mm(grads[1], proj_ref[1])
    partial = (total + mm(grads[2], proj_ref[2])).astype(BF)
    to_wire([partial, out], back_ref, wire_ref)


def temporal_return(arrived_ref, partial_ref, heads_ref, held_ref):
    widths = partial_ref.shape[1], heads_ref.shape[1]
    partial, heads = from_wire(arrived_ref, held_ref, widths)
    partial_ref[...] = partial.astype(BF)
    heads_ref[...] = heads.astype(BF)


def mix_temporal(heads_ref, out_ref, mixed_ref):
    mixed_ref[...] = mm(heads_ref[...], out_ref[...]).astype(BF)


def middle_back(
    place_ref, cot_ref, middle_ref, mod_ref, mine_ref, other_ref, b0, b1, b2, b3, scaled_ref, grad_ref,
    held_ref,
):
    incoming = mine_ref[...].astype(F32) + other_ref[...].astype(F32)
    grad = cot_ref[...].astype(F32) + norm_back(middle_ref[...], mod_ref[4], incoming)
    scaled = (mod_ref[2] * grad).astype(BF)
    for block, ref in zip(split_columns(scaled, place_ref[0], held_ref), (b0, b1, b2, b3)):
        ref[...] = block
    scaled_ref[...] = scaled
    grad_ref[...] = grad


def spatial_back(scaled_ref, out_ref, packed_ref, weights_ref, proj_ref, partial_ref):
    grad_heads = mm_rt(scaled_ref[...], out_ref[...]).astype(BF)
    grads = attend_back(
        packed_ref[0], packed_ref[1], packed_ref[2], grad_heads, weights_ref[...]
    )
    total = mm(grads[0], proj_ref[0]) + mm(grads[1], proj_ref[1])
    partial_ref[...] = (total + mm(grads[2], proj_ref[2])).astype(BF)


def latent_step(x_ref, mod_ref, grad_ref, mine_ref, other_ref, latent_ref):
    incoming = mine_ref[...].astype(F32) + other_ref[...].astype(F32)
    latent_ref[...] = grad_ref[...] + norm_back(x_ref[...].astype(F32), mod_ref[1], incoming)


def output_step(middle_ref, mod_ref, mine_ref, other_ref, block_ref):
    mixed = mine_ref[...].astype(F32) + other_ref[...].astype(F32)
    block_ref[...] = (middle_ref[...] + mod_ref[5] * mixed).astype(BF)


def product_of(refs):
    total = 0.0
    for i in range(DP):
        total = total + mm_lt(refs[i][...], refs[DP + i][...])
    return total


def temporal_product(*refs):
    refs[-1][...] = product_of(refs[:-1])


def weight_products(*refs):
    temporal_ref, wire_ref, tiles_ref, held_ref = refs[2 * DP :]
    totals = (product_of(refs[: 2 * DP]), temporal_ref[...])
    rows, columns = totals[0].shape
    whole = columns // LANES * LANES
    tiles = [total[:, at : at + LANES] for total in totals for at in range(0, whole, LANES)]
    tiles.append(jnp.concatenate([total[:, whole:] for total in totals], axis=1))
    for i, tile in enumerate(tiles):
        tiles_ref[i * rows : (i + 1) * rows] = tile
    part = rows // SEQ
    slots = held_ref.shape[0] // SEQ
    for slot in range(slots):
        tile, row = slot // part, slot % part
        if tile < len(tiles):
            taken = tiles_ref[pl.ds(tile * rows + row, SEQ, stride=part), :]
        else:
            taken = jnp.zeros((SEQ, LANES), F32)
        held_ref[pl.ds(slot, SEQ, stride=slots), :] = taken
    wire_ref[...] = held_ref[...].astype(BF)


def weight_sums(arrived_ref, spatial_ref, temporal_ref):
    slots = arrived_ref.shape[0] // SEQ
    total = arrived_ref[:slots].astype(F32)
    for i in range(1, SEQ):
        total = total + arrived_ref[i * slots : (i + 1) * slots].astype(F32)
    part, columns = spatial_ref.shape
    whole = columns // LANES * LANES
    at = 0
    for ref in (spatial_ref, temporal_ref):
        for start in range(0, whole, LANES):
            ref[:, start : start + LANES] = total[at : at + part]
            at += part
    spatial_ref[:, whole:] = total[at : at + part, : columns - whole]
    temporal_ref[:, whole:] = total[at : at + part, columns - whole :]


class Late:
    def __init__(self, source, target, sems):
        self.target = target
        self.shape = target.shape
        parts = self.shape[0] if len(self.shape) == 3 and self.shape[0] == 3 else 0
        self.parts = parts
        if parts:
            self.copies = [
                pltpu.make_async_copy(source.at[i], target.at[i], sems.at[i]) for i in range(parts)
            ]
        else:
            self.copies = [pltpu.make_async_copy(source, target, sems.at[0])]
        self.waiting = [True] * len(self.copies)
        for copy in self.copies:
            copy.start()

    def wait(self, wanted):
        for i in wanted:
            if self.waiting[i]:
                self.copies[i].wait()
                self.waiting[i] = False

    def __getitem__(self, index):
        one = self.parts and isinstance(index, int)
        self.wait([index] if one else range(len(self.copies)))
        return self.target[index]


class Early:
    def __init__(self, source, target, sem):
        self.source = source
        self.shape = source.shape
        self.dtype = source.dtype
        self.copy = pltpu.make_async_copy(source, target, sem)
        self.started = False

    def start(self):
        if not self.started:
            self.copy.start()
            self.started = True

    def __setitem__(self, index, value):
        self.source[index] = value
        if index is Ellipsis:
            self.start()


def call(body, outs, *operands, scalars=0, scratch=(), flops=0, manual=False, vmem=0):
    smem, whole = [pl.BlockSpec(memory_space=space) for space in (pltpu.SMEM, pltpu.VMEM)]
    apart = pl.BlockSpec(memory_space=pl.ANY) if manual else whole
    count = len(operands)
    late = range(scalars, count) if manual else ()
    early = range(len(outs)) if manual else ()
    specs = [smem if i < scalars else apart for i in range(count)]
    shapes = [jax.ShapeDtypeStruct(shape, dtype) for shape, dtype in outs]
    out_specs = [apart] * len(outs)
    moved = sum(x.size * x.dtype.itemsize for x in [*operands, *shapes])
    held = [pltpu.VMEM(operands[i].shape, operands[i].dtype) for i in late]
    held += [pltpu.VMEM(shapes[i].shape, shapes[i].dtype) for i in early]
    sems = [pltpu.SemaphoreType.DMA((3,))] * len(late) + [pltpu.SemaphoreType.DMA] * len(early)
    own = list(scratch)

    def wrapped(*refs):
        refs = list(refs)
        extra = refs[count + len(outs) :]
        buffers, marks = extra[len(own) : len(own) + len(held)], extra[len(own) + len(held) :]
        for n, i in enumerate(late):
            refs[i] = Late(refs[i], buffers[n], marks[n])
        results = []
        for n, i in enumerate(early):
            at = len(late) + n
            refs[count + i] = Early(buffers[at], refs[count + i], marks[at])
            results.append(refs[count + i])
        body(*refs[: count + len(outs)], *extra[: len(own)])
        for result in results:
            result.start()
        for result in results:
            result.copy.wait()

    single = len(shapes) == 1
    return pl.pallas_call(
        wrapped,
        out_shape=shapes[0] if single else shapes,
        in_specs=specs,
        out_specs=out_specs[0] if single else out_specs,
        scratch_shapes=own + held + sems,
        cost_estimate=pl.CostEstimate(flops=flops, bytes_accessed=moved, transcendentals=0),
        compiler_params=pltpu.CompilerParams(vmem_limit_bytes=(vmem or (60 if manual else 40)) * 1024 * 1024),
    )(*operands)


def swap_pair(array):
    return lax.ppermute(array, "tensor", PAIR)


def swap_both(array, dp_mask, seq_mask):
    if not seq_mask:
        return swap_dp(array, dp_mask)
    if not dp_mask:
        return lax.ppermute(array, "seq", [(i, i ^ seq_mask) for i in range(SEQ)])
    mask = dp_mask * SEQ + seq_mask
    return lax.ppermute(array, ("dp", "seq"), [(i, i ^ mask) for i in range(DP * SEQ)])


def swap_near(array, index):
    return swap_both(array, index % 2, Z_RING * (index // 2))


def swap_dp(array, mask):
    return lax.ppermute(array, "dp", [(i, i ^ mask) for i in range(DP)])


def all_to_all(array):
    rows, width = array.shape
    cut = array.reshape(SEQ, rows // SEQ, width)
    moved = lax.all_to_all(cut, "seq", split_axis=0, concat_axis=0, tiled=True)
    return moved.reshape(rows, width)


def per_device(
    latents, modulation, cotangent, proj_spatial, out_spatial, proj_temporal, out_temporal
):
    tokens, width = latents.shape[-2:]
    local = out_spatial.shape[1]
    heads = local // HEAD_DIM
    x = latents.reshape(tokens, width)
    cot = cotangent.reshape(tokens, width)
    mod = modulation.transpose(1, 0, 2)
    proj_s = proj_spatial.transpose(1, 2, 0)
    proj_t = proj_temporal.transpose(1, 2, 0)
    out_s = out_spatial.T
    out_t = out_temporal.T
    dp, seq = lax.axis_index("dp"), lax.axis_index("seq")
    x_low = seq // Z_RING % 2
    near_place = (2 * x_low + dp % 2).astype(jnp.int32).reshape(1)
    wide = ((tokens, width), BF)
    narrow = ((tokens, local), BF)
    full = ((tokens, width), F32)
    block = ((tokens, width // DP), BF)
    blocks_held = pltpu.VMEM((DP, tokens, width // DP), BF)
    slots = wire_slots(4 * local)
    wire = ((SEQ * slots, LANES), BF)
    wire_held = pltpu.VMEM((SEQ * slots, LANES), F32)
    slots = wire_slots(width + local)
    back = ((SEQ * slots, LANES), BF)
    back_held = pltpu.VMEM((SEQ * slots, LANES), F32)
    product = 2 * tokens * width * local
    attention = 4 * heads * tokens * tokens * local

    packed_s, weights_s, heads_s, mixed_s = call(
        spatial_forward,
        [((3, tokens, local), BF), ((heads * tokens, tokens), F32), narrow, wide],
        x, mod, proj_s, out_s, manual=True, flops=4 * product + attention,
    )
    mixed_other = swap_pair(mixed_s)
    grad_heads_t, *blocks_t = call(
        upstream_start, [narrow] + [block] * DP,
        near_place, cot, mod, out_t, x, proj_t, scalars=1, scratch=[blocks_held], flops=product,
    )
    heads_x = swap_near(heads_s, 2)
    heads_core = swap_near(heads_s, 1)
    mixed_other, heads_x, heads_core = lax.optimization_barrier((mixed_other, heads_x, heads_core))
    wire_out, middle = call(
        middle_step, [wire, full],
        x, mixed_s, mixed_other, mod, grad_heads_t, proj_t, scratch=[wire_held],
        flops=4 * product,
    )
    heads_s = [heads_s, heads_core, heads_x, swap_near(heads_x, 1)]
    blocks_t = [blocks_t[0]] + [swap_near(blocks_t[i], i) for i in range(1, DP)]
    arrived = all_to_all(wire_out)
    wire_back = call(
        temporal_step, [back], arrived, proj_t, manual=True, vmem=40, scratch=[wire_held, back_held],
        flops=3 * product + 6 * attention,
    )
    returned = all_to_all(wire_back)
    returned, heads_s, blocks_t = lax.optimization_barrier((returned, heads_s, blocks_t))
    partial_t, heads_t = call(
        temporal_return, [wide, narrow], returned, scratch=[back_held]
    )
    partial_other = swap_pair(partial_t)
    heads_near = [swap_near(heads_t, 1), swap_near(heads_t, 2)]
    heads_near.append(swap_near(heads_near[1], 1))
    partial_other, heads_near[1] = lax.optimization_barrier((partial_other, heads_near[1]))
    *blocks_s, scaled_s, grad_middle = call(
        middle_back, [block] * DP + [wide, full],
        near_place, cot, middle, mod, partial_t, partial_other, scalars=1, scratch=[blocks_held],
    )
    blocks_s = [blocks_s[0]] + [swap_near(blocks_s[i], i) for i in range(1, DP)]
    partial_s = call(
        spatial_back, [wide],
        scaled_s, out_s, packed_s, weights_s, proj_s, manual=True,
        flops=4 * product + 5 * attention,
    )
    partial_s_other = swap_pair(partial_s)
    temporal_sum = call(
        temporal_product, [((width // DP, local), F32)], *blocks_t, heads_t, *heads_near, manual=True,
        flops=2 * product, vmem=60,
    )
    heads_late, _ = lax.optimization_barrier((heads_t, blocks_s[0]))
    mixed_t = call(mix_temporal, [wide], heads_late, out_t, flops=product)
    mixed_t_other = swap_pair(mixed_t)
    temporal_sum, mixed_t_other = lax.optimization_barrier((temporal_sum, mixed_t_other))
    slots = wire_slots(2 * width // DP // SEQ * local // QUARTERS)
    sums = call(
        weight_products, [((SEQ * slots, LANES), BF)],
        *blocks_s, *heads_s, temporal_sum, manual=True, flops=2 * product, vmem=60,
        scratch=[
            pltpu.VMEM((2 * local // LANES * width // DP, LANES), F32),
            pltpu.VMEM((SEQ * slots, LANES), F32),
        ],
    )
    sums = lax.all_to_all(
        sums.reshape(SEQ, slots, LANES), ("dp", "seq"), split_axis=0, concat_axis=0, tiled=True,
        axis_index_groups=FAR_GROUPS,
    ).reshape(SEQ * slots, LANES)
    block_output = call(output_step, [wide], middle, mod, mixed_t, mixed_t_other)
    latent_grad = call(latent_step, [full], x, mod, grad_middle, partial_s, partial_s_other)
    part = ((width // DP // SEQ, local), F32)
    grad_out_s, grad_out_t = call(weight_sums, [part, part], sums)
    return (
        block_output.reshape(latents.shape),
        latent_grad.reshape(latents.shape),
        grad_out_s,
        grad_out_t,
    )


def solution(mesh):
    placed = (
        P("dp", "seq", None, None),
        P("dp", None, None),
        P("dp", "seq", None, None),
        P(None, None, "tensor"),
        P(None, "tensor"),
        P(None, None, "tensor"),
        P(None, "tensor"),
    )
    return jax.shard_map(
        per_device,
        mesh=mesh,
        in_specs=placed,
        out_specs=(
            P("dp", "seq", None, None),
            P("dp", "seq", None, None),
            P(("dp", "seq"), "tensor"),
            P(("dp", "seq"), "tensor"),
        ),
        check_vma=False,
    )
```

```python
import functools

import jax
import jax.numpy as jnp
from jax import lax
from jax.experimental import pallas as pl
from jax.experimental.pallas import tpu as pltpu
from jax.sharding import PartitionSpec as P

HEAD_DIM = 72
NORM_EPS = 1e-06
PAIR = ((0, 1), (1, 0))
DP = 4
SEQ = 32
BF = jnp.bfloat16
F32 = jnp.float32
X_RING = 4
Z_RING = 8
Z_GROUPS = tuple(tuple(z + Z_RING * x for z in range(Z_RING)) for x in range(X_RING))
ROWS = 9


def mm(left, right):
    return jnp.dot(left, right, preferred_element_type=F32)


def mm_rt(left, right):
    return lax.dot_general(left, right, (((1,), (1,)), ((), ())), preferred_element_type=F32)


def mm_lt(left, right):
    return lax.dot_general(left, right, (((0,), (0,)), ((), ())), preferred_element_type=F32)


def normalise(values):
    average = jnp.mean(values, axis=-1, keepdims=True)
    centred = values - average
    inverse = lax.rsqrt(jnp.mean(centred * centred, axis=-1, keepdims=True) + NORM_EPS)
    return centred * inverse, inverse


def norm_back(values, scale_row, incoming):
    unit, inverse = normalise(values)
    scaled = incoming * (1.0 + scale_row)
    mean_plain = jnp.mean(scaled, axis=-1, keepdims=True)
    mean_unit = jnp.mean(scaled * unit, axis=-1, keepdims=True)
    return inverse * (scaled - mean_plain - unit * mean_unit)


def stack_heads(values):
    width = values.shape[1]
    owner = lax.broadcasted_iota(jnp.int32, (1, width), 1) // HEAD_DIM
    parts = [values * (owner == head).astype(F32).astype(BF) for head in range(width // HEAD_DIM)]
    return jnp.concatenate(parts, axis=0)


def side_by_side(stacked):
    tokens = stacked.shape[1]
    heads = stacked.shape[0] // tokens
    return jnp.concatenate([stacked[h * tokens : (h + 1) * tokens] for h in range(heads)], axis=1)


def softmax_weights(queries, keys_in, same=None):
    scores = mm_rt(stack_heads(queries), keys_in) * HEAD_DIM**-0.5
    if same is not None:
        scores = jnp.where(same, scores, -1e30)
    raised = jnp.exp(scores - jnp.max(scores, axis=-1, keepdims=True))
    return raised / jnp.sum(raised, axis=-1, keepdims=True)


def attend_back(queries, keys_in, values_in, grad_out, weights):
    grad_stacked = stack_heads(grad_out)
    grad_weights = mm_rt(grad_stacked, values_in)
    inner_sum = jnp.sum(grad_weights * weights, axis=-1, keepdims=True)
    grad_scores = (weights * (grad_weights - inner_sum) * HEAD_DIM**-0.5).astype(BF)
    grad_queries = mm(side_by_side(grad_scores), stack_heads(keys_in)).astype(BF)
    grad_keys = mm_lt(grad_scores, stack_heads(queries)).astype(BF)
    grad_values = mm_lt(weights.astype(BF), grad_stacked).astype(BF)
    return grad_queries, grad_keys, grad_values


FAR_GROUPS = tuple(
    tuple(((2 * far + core) * X_RING + 2 * x_high + x_low) * Z_RING + z for far in range(2) for x_high in range(2))
    for core in range(2)
    for x_low in range(2)
    for z in range(Z_RING)
)
LANES = 128
QUARTERS = 4


def wire_slots(columns):
    slots = QUARTERS * columns // LANES
    return -(-slots // 8) * 8


def wire_pieces(columns):
    pieces, slot = [], 0
    for start in range(0, columns, LANES):
        wide = min(LANES, columns - start)
        for quarter in range(QUARTERS if wide == LANES else QUARTERS // 2):
            pieces.append((slot, start, wide, quarter))
            slot += 1
    return pieces, slot


def to_wire(arrays, held_ref, wire_ref):
    devices = arrays[0].shape[0] // QUARTERS
    slots = held_ref.shape[0] // devices
    base = 0
    for values in arrays:
        values = values.astype(F32)
        pieces, used = wire_pieces(values.shape[1])
        for slot, start, wide, quarter in pieces:
            part = values[quarter * devices : (quarter + 1) * devices, start : start + wide]
            if wide < LANES:
                later = (quarter + 2) * devices
                other = values[later : later + devices, start : start + wide]
                part = jnp.concatenate([part, other], axis=1)
            held_ref[pl.ds(base + slot, devices, stride=slots), :] = part
        base += used
    for slot in range(base, slots):
        held_ref[pl.ds(slot, devices, stride=slots), :] = jnp.zeros((devices, LANES), F32)
    wire_ref[...] = held_ref[...].astype(BF)


def from_wire(wire_ref, held_ref, widths):
    devices = SEQ
    slots = held_ref.shape[0] // devices
    held_ref[...] = wire_ref[...].astype(F32)
    base = 0
    arrays = []
    for columns in widths:
        pieces, used = wire_pieces(columns)
        tiles = {}
        for slot, start, wide, quarter in pieces:
            part = held_ref[pl.ds(base + slot, devices, stride=slots), :]
            if wide < LANES:
                tiles[start, quarter] = part[:, :wide]
                tiles[start, quarter + 2] = part[:, wide:]
            else:
                tiles[start, quarter] = part
        base += used
        starts = sorted({start for start, _ in tiles})
        columns_of = [
            jnp.concatenate([tiles[start, quarter] for quarter in range(QUARTERS)], axis=0)
            for start in starts
        ]
        arrays.append(jnp.concatenate(columns_of, axis=1))
    return arrays


def spatial_forward(
    x_ref, mod_ref, proj_ref, out_ref, packed_ref, weights_ref, heads_ref, mixed_ref
):
    unit, _ = normalise(x_ref[...].astype(F32))
    normed = (unit * (1.0 + mod_ref[1]) + mod_ref[0]).astype(BF)
    parts = []
    for i in range(3):
        parts.append(mm_rt(normed, proj_ref[i]).astype(BF))
        packed_ref[i] = parts[i]
    queries, keys_in, values_in = parts
    weights = softmax_weights(queries, keys_in)
    weights_ref[...] = weights
    heads = mm(side_by_side(weights.astype(BF)), stack_heads(values_in)).astype(BF)
    heads_ref[...] = heads
    mixed_ref[...] = mm(heads, out_ref[...]).astype(BF)


def split_columns(scaled, place, held_ref):
    piece = scaled.shape[1] // (DP * X_RING)
    for x_low in range(2):
        for core in range(2):
            starts = [
                ((far * 2 + core) * X_RING + x_high * 2 + x_low) * piece
                for far in range(2)
                for x_high in range(2)
            ]
            parts = [scaled[:, start : start + piece] for start in starts]
            held_ref[2 * x_low + core] = jnp.concatenate(parts, axis=1)
    return [held_ref[place ^ i] for i in range(DP)]


def upstream_start(
    place_ref, cot_ref, mod_ref, out_ref, x_ref, proj_ref, grad_ref, b0, b1, b2, b3, held_ref
):
    del x_ref, proj_ref
    scaled = (mod_ref[5] * cot_ref[...].astype(F32)).astype(BF)
    grad_ref[...] = mm_rt(scaled, out_ref[...]).astype(BF)
    for block, ref in zip(split_columns(scaled, place_ref[0], held_ref), (b0, b1, b2, b3)):
        ref[...] = block


def middle_step(
    x_ref, mine_ref, other_ref, mod_ref, grad_ref, proj_ref, wire_ref, middle_ref, held_ref
):
    mixed = mine_ref[...].astype(F32) + other_ref[...].astype(F32)
    middle = x_ref[...].astype(F32) + mod_ref[2] * mixed
    middle_ref[...] = middle
    unit, _ = normalise(middle)
    normed = (unit * (1.0 + mod_ref[4]) + mod_ref[3]).astype(BF)
    parts = [mm_rt(normed, proj_ref[i]).astype(BF) for i in range(3)]
    to_wire(parts + [grad_ref[...]], held_ref, wire_ref)


def temporal_step(arrived_ref, proj_ref, wire_ref, held_ref, back_ref):
    local = arrived_ref.shape[0] * LANES // (QUARTERS * SEQ) // 4
    parts = from_wire(arrived_ref, held_ref, (local,) * 4)
    queries, keys_in, values_in, grad_out = [part.astype(BF) for part in parts]
    tokens = queries.shape[0]
    frames = tokens // QUARTERS
    stacked = (local // HEAD_DIM * tokens, tokens)
    row = lax.broadcasted_iota(jnp.int32, stacked, 0) % tokens
    column = lax.broadcasted_iota(jnp.int32, stacked, 1)
    weights = softmax_weights(queries, keys_in, row // frames == column // frames)
    out = mm(side_by_side(weights.astype(BF)), stack_heads(values_in)).astype(BF)
    grads = attend_back(queries, keys_in, values_in, grad_out, weights)
    total = mm(grads[0], proj_ref[0]) + mm(grads[1], proj_ref[1])
    partial = (total + mm(grads[2], proj_ref[2])).astype(BF)
    to_wire([partial, out], back_ref, wire_ref)


def temporal_return(arrived_ref, partial_ref, heads_ref, held_ref):
    widths = partial_ref.shape[1], heads_ref.shape[1]
    partial, heads = from_wire(arrived_ref, held_ref, widths)
    partial_ref[...] = partial.astype(BF)
    heads_ref[...] = heads.astype(BF)


def mix_temporal(heads_ref, out_ref, mixed_ref):
    mixed_ref[...] = mm(heads_ref[...], out_ref[...]).astype(BF)


def middle_back(
    place_ref, cot_ref, middle_ref, mod_ref, mine_ref, other_ref, b0, b1, b2, b3, scaled_ref, grad_ref,
    held_ref,
):
    incoming = mine_ref[...].astype(F32) + other_ref[...].astype(F32)
    grad = cot_ref[...].astype(F32) + norm_back(middle_ref[...], mod_ref[4], incoming)
    scaled = (mod_ref[2] * grad).astype(BF)
    for block, ref in zip(split_columns(scaled, place_ref[0], held_ref), (b0, b1, b2, b3)):
        ref[...] = block
    scaled_ref[...] = scaled
    grad_ref[...] = grad


def spatial_back(scaled_ref, out_ref, packed_ref, weights_ref, proj_ref, partial_ref):
    grad_heads = mm_rt(scaled_ref[...], out_ref[...]).astype(BF)
    grads = attend_back(
        packed_ref[0], packed_ref[1], packed_ref[2], grad_heads, weights_ref[...]
    )
    total = mm(grads[0], proj_ref[0]) + mm(grads[1], proj_ref[1])
    partial_ref[...] = (total + mm(grads[2], proj_ref[2])).astype(BF)


def latent_step(x_ref, mod_ref, grad_ref, mine_ref, other_ref, latent_ref):
    incoming = mine_ref[...].astype(F32) + other_ref[...].astype(F32)
    latent_ref[...] = grad_ref[...] + norm_back(x_ref[...].astype(F32), mod_ref[1], incoming)


def output_step(middle_ref, mod_ref, mine_ref, other_ref, block_ref):
    mixed = mine_ref[...].astype(F32) + other_ref[...].astype(F32)
    block_ref[...] = (middle_ref[...] + mod_ref[5] * mixed).astype(BF)


def product_of(refs):
    total = 0.0
    for i in range(DP):
        total = total + mm_lt(refs[i][...], refs[DP + i][...])
    return total


def temporal_product(*refs):
    refs[-1][...] = product_of(refs[:-1])


def weight_products(*refs):
    temporal_ref, wire_ref = refs[2 * DP :]
    totals = (product_of(refs[: 2 * DP]), temporal_ref[...])
    rows, columns = totals[0].shape
    whole = columns // LANES * LANES
    tiles = [total[:, at : at + LANES] for total in totals for at in range(0, whole, LANES)]
    tiles.append(jnp.concatenate([total[:, whole:] for total in totals], axis=1))
    cut = rows // DP
    for i in range(DP):
        chunk = [tile[i * cut : (i + 1) * cut] for tile in tiles]
        wire_ref[i] = jnp.concatenate(chunk, axis=0).astype(BF)


def add_sources(parts):
    total = parts[0].astype(F32)
    for part in parts[1:]:
        total = total + part.astype(F32)
    return total


def weight_halfway(arrived_ref, wire_ref, total_ref, held_ref):
    total_ref[...] = add_sources([arrived_ref[i] for i in range(DP)])
    slots = held_ref.shape[0] // Z_RING
    part = ROWS
    for slot in range(slots):
        tile, row = slot // part, slot % part
        start = tile * part * Z_RING + row
        if start < total_ref.shape[0]:
            taken = total_ref[pl.ds(start, Z_RING, stride=part), :]
        else:
            taken = jnp.zeros((Z_RING, LANES), F32)
        held_ref[pl.ds(slot, Z_RING, stride=slots), :] = taken
    wire_ref[...] = held_ref[...].astype(BF)


def weight_sums(arrived_ref, spatial_ref, temporal_ref):
    slots = arrived_ref.shape[0] // Z_RING
    total = arrived_ref[:slots].astype(F32)
    for i in range(1, Z_RING):
        total = total + arrived_ref[i * slots : (i + 1) * slots].astype(F32)
    part, columns = spatial_ref.shape
    whole = columns // LANES * LANES
    at = 0
    for ref in (spatial_ref, temporal_ref):
        for start in range(0, whole, LANES):
            ref[:, start : start + LANES] = total[at : at + part]
            at += part
    spatial_ref[:, whole:] = total[at : at + part, : columns - whole]
    temporal_ref[:, whole:] = total[at : at + part, columns - whole :]


class Late:
    def __init__(self, source, target, sems):
        self.target = target
        self.shape = target.shape
        parts = self.shape[0] if len(self.shape) == 3 and self.shape[0] == 3 else 0
        self.parts = parts
        if parts:
            self.copies = [
                pltpu.make_async_copy(source.at[i], target.at[i], sems.at[i]) for i in range(parts)
            ]
        else:
            self.copies = [pltpu.make_async_copy(source, target, sems.at[0])]
        self.waiting = [True] * len(self.copies)
        for copy in self.copies:
            copy.start()

    def wait(self, wanted):
        for i in wanted:
            if self.waiting[i]:
                self.copies[i].wait()
                self.waiting[i] = False

    def __getitem__(self, index):
        one = self.parts and isinstance(index, int)
        self.wait([index] if one else range(len(self.copies)))
        return self.target[index]


class Early:
    def __init__(self, source, target, sem):
        self.source = source
        self.shape = source.shape
        self.dtype = source.dtype
        self.copy = pltpu.make_async_copy(source, target, sem)
        self.started = False

    def start(self):
        if not self.started:
            self.copy.start()
            self.started = True

    def __setitem__(self, index, value):
        self.source[index] = value
        if index is Ellipsis:
            self.start()


def call(body, outs, *operands, scalars=0, scratch=(), flops=0, manual=False, vmem=0):
    smem, whole = [pl.BlockSpec(memory_space=space) for space in (pltpu.SMEM, pltpu.VMEM)]
    apart = pl.BlockSpec(memory_space=pl.ANY) if manual else whole
    count = len(operands)
    late = range(scalars, count) if manual else ()
    early = range(len(outs)) if manual else ()
    specs = [smem if i < scalars else apart for i in range(count)]
    shapes = [jax.ShapeDtypeStruct(shape, dtype) for shape, dtype in outs]
    out_specs = [apart] * len(outs)
    moved = sum(x.size * x.dtype.itemsize for x in [*operands, *shapes])
    held = [pltpu.VMEM(operands[i].shape, operands[i].dtype) for i in late]
    held += [pltpu.VMEM(shapes[i].shape, shapes[i].dtype) for i in early]
    sems = [pltpu.SemaphoreType.DMA((3,))] * len(late) + [pltpu.SemaphoreType.DMA] * len(early)
    own = list(scratch)

    def wrapped(*refs):
        refs = list(refs)
        extra = refs[count + len(outs) :]
        buffers, marks = extra[len(own) : len(own) + len(held)], extra[len(own) + len(held) :]
        for n, i in enumerate(late):
            refs[i] = Late(refs[i], buffers[n], marks[n])
        results = []
        for n, i in enumerate(early):
            at = len(late) + n
            refs[count + i] = Early(buffers[at], refs[count + i], marks[at])
            results.append(refs[count + i])
        body(*refs[: count + len(outs)], *extra[: len(own)])
        for result in results:
            result.start()
        for result in results:
            result.copy.wait()

    single = len(shapes) == 1
    return pl.pallas_call(
        wrapped,
        out_shape=shapes[0] if single else shapes,
        in_specs=specs,
        out_specs=out_specs[0] if single else out_specs,
        scratch_shapes=own + held + sems,
        cost_estimate=pl.CostEstimate(flops=flops, bytes_accessed=moved, transcendentals=0),
        compiler_params=pltpu.CompilerParams(vmem_limit_bytes=(vmem or (60 if manual else 32)) * 1024 * 1024),
    )(*operands)


def swap_pair(array):
    return lax.ppermute(array, "tensor", PAIR)


def swap_both(array, dp_mask, seq_mask):
    if not seq_mask:
        return swap_dp(array, dp_mask)
    if not dp_mask:
        return lax.ppermute(array, "seq", [(i, i ^ seq_mask) for i in range(SEQ)])
    mask = dp_mask * SEQ + seq_mask
    return lax.ppermute(array, ("dp", "seq"), [(i, i ^ mask) for i in range(DP * SEQ)])


def swap_near(array, index):
    return swap_both(array, index % 2, Z_RING * (index // 2))


def swap_dp(array, mask):
    return lax.ppermute(array, "dp", [(i, i ^ mask) for i in range(DP)])


def all_to_all(array):
    rows, width = array.shape
    cut = array.reshape(SEQ, rows // SEQ, width)
    moved = lax.all_to_all(cut, "seq", split_axis=0, concat_axis=0, tiled=True)
    return moved.reshape(rows, width)


def group_all_to_all(array, groups):
    return lax.all_to_all(
        array, "seq", split_axis=0, concat_axis=0, tiled=True, axis_index_groups=groups
    )


def per_device(
    latents, modulation, cotangent, proj_spatial, out_spatial, proj_temporal, out_temporal
):
    tokens, width = latents.shape[-2:]
    local = out_spatial.shape[1]
    heads = local // HEAD_DIM
    x = latents.reshape(tokens, width)
    cot = cotangent.reshape(tokens, width)
    mod = modulation.transpose(1, 0, 2)
    proj_s = proj_spatial.transpose(1, 2, 0)
    proj_t = proj_temporal.transpose(1, 2, 0)
    out_s = out_spatial.T
    out_t = out_temporal.T
    dp, seq = lax.axis_index("dp"), lax.axis_index("seq")
    x_low = seq // Z_RING % 2
    near_place = (2 * x_low + dp % 2).astype(jnp.int32).reshape(1)
    wide = ((tokens, width), BF)
    narrow = ((tokens, local), BF)
    full = ((tokens, width), F32)
    block = ((tokens, width // DP), BF)
    blocks_held = pltpu.VMEM((DP, tokens, width // DP), BF)
    slots = wire_slots(4 * local)
    wire = ((SEQ * slots, LANES), BF)
    wire_held = pltpu.VMEM((SEQ * slots, LANES), F32)
    slots = wire_slots(width + local)
    back = ((SEQ * slots, LANES), BF)
    back_held = pltpu.VMEM((SEQ * slots, LANES), F32)
    product = 2 * tokens * width * local
    attention = 4 * heads * tokens * tokens * local

    packed_s, weights_s, heads_s, mixed_s = call(
        spatial_forward,
        [((3, tokens, local), BF), ((heads * tokens, tokens), F32), narrow, wide],
        x, mod, proj_s, out_s, manual=True, flops=4 * product + attention,
    )
    mixed_other = swap_pair(mixed_s)
    grad_heads_t, *blocks_t = call(
        upstream_start, [narrow] + [block] * DP,
        near_place, cot, mod, out_t, x, proj_t, scalars=1, scratch=[blocks_held], flops=product,
    )
    heads_x = swap_near(heads_s, 2)
    heads_core = swap_near(heads_s, 1)
    mixed_other, heads_x, heads_core = lax.optimization_barrier((mixed_other, heads_x, heads_core))
    wire_out, middle = call(
        middle_step, [wire, full],
        x, mixed_s, mixed_other, mod, grad_heads_t, proj_t, scratch=[wire_held],
        flops=4 * product,
    )
    heads_s = [heads_s, heads_core, heads_x, swap_near(heads_x, 1)]
    blocks_t = [blocks_t[0]] + [swap_near(blocks_t[i], i) for i in range(1, DP)]
    arrived = all_to_all(wire_out)
    wire_back = call(
        temporal_step, [back], arrived, proj_t, manual=True, vmem=40, scratch=[wire_held, back_held],
        flops=3 * product + 6 * attention,
    )
    returned = all_to_all(wire_back)
    returned, heads_s, blocks_t = lax.optimization_barrier((returned, heads_s, blocks_t))
    partial_t, heads_t = call(
        temporal_return, [wide, narrow], returned, scratch=[back_held]
    )
    partial_other = swap_pair(partial_t)
    heads_near = [swap_near(heads_t, 1), swap_near(heads_t, 2)]
    heads_near.append(swap_near(heads_near[1], 1))
    partial_other, heads_near[1] = lax.optimization_barrier((partial_other, heads_near[1]))
    *blocks_s, scaled_s, grad_middle = call(
        middle_back, [block] * DP + [wide, full],
        near_place, cot, middle, mod, partial_t, partial_other, scalars=1, scratch=[blocks_held],
    )
    blocks_s = [blocks_s[0]] + [swap_near(blocks_s[i], i) for i in range(1, DP)]
    temporal_sum = call(
        temporal_product, [((width // DP, local), F32)], *blocks_t, heads_t, *heads_near, manual=True,
        flops=2 * product, vmem=60,
    )
    heads_late, _ = lax.optimization_barrier((heads_t, blocks_s[0]))
    mixed_t = call(mix_temporal, [wide], heads_late, out_t, flops=product)
    mixed_t_other = swap_pair(mixed_t)
    temporal_sum, mixed_t_other = lax.optimization_barrier((temporal_sum, mixed_t_other))
    tiled = 2 * local // LANES * width // DP // DP
    piece = ((DP, tiled, LANES), BF)
    slots = wire_slots(2 * ROWS * local // QUARTERS)
    sums = call(
        weight_products, [piece], *blocks_s, *heads_s, temporal_sum, manual=True, flops=2 * product,
    )
    scaled_s, sums = lax.optimization_barrier((scaled_s, sums))
    partial_s = call(
        spatial_back, [wide],
        scaled_s, out_s, packed_s, weights_s, proj_s, manual=True,
        flops=4 * product + 5 * attention,
    )
    partial_s_other = swap_pair(partial_s)
    sums = lax.all_to_all(
        sums, ("dp", "seq"), split_axis=0, concat_axis=0, tiled=True, axis_index_groups=FAR_GROUPS
    )
    sums, partial_s = lax.optimization_barrier((sums, partial_s))
    sums_half = call(
        weight_halfway, [((Z_RING * slots, LANES), BF)], sums,
        scratch=[pltpu.VMEM((tiled, LANES), F32), pltpu.VMEM((Z_RING * slots, LANES), F32)],
    )
    sums_in = group_all_to_all(sums_half.reshape(Z_RING, slots, LANES), Z_GROUPS)
    sums_in = sums_in.reshape(Z_RING * slots, LANES)
    block_output = call(output_step, [wide], middle, mod, mixed_t, mixed_t_other)
    latent_grad = call(latent_step, [full], x, mod, grad_middle, partial_s, partial_s_other)
    part = ((width // DP // SEQ, local), F32)
    grad_out_s, grad_out_t = call(weight_sums, [part, part], sums_in)
    return (
        block_output.reshape(latents.shape),
        latent_grad.reshape(latents.shape),
        grad_out_s,
        grad_out_t,
    )


def solution(mesh):
    placed = (
        P("dp", "seq", None, None),
        P("dp", None, None),
        P("dp", "seq", None, None),
        P(None, None, "tensor"),
        P(None, "tensor"),
        P(None, None, "tensor"),
        P(None, "tensor"),
    )
    return jax.shard_map(
        per_device,
        mesh=mesh,
        in_specs=placed,
        out_specs=(
            P("dp", "seq", None, None),
            P("dp", "seq", None, None),
            P(("dp", "seq"), "tensor"),
            P(("dp", "seq"), "tensor"),
        ),
        check_vma=False,
    )
```
